128 devices in a mesh: row: 16 (over x_hi, y, core), col: 8 (over z, x_lo).
Axes of the slice: x: 4 (x_hi: 2, x_lo: 2; x = x_hi * 2 + x_lo), y: 4, z: 4, core: 2. Of those that a mesh axis runs over, the one named last changes fastest.
Arguments:
- pair_rep: bfloat16 [1152, 1152, 128], P('row', 'col'), may hold values from -6 to 6
- norm_gain: float32 [128], replicated, may hold values from 0.1 to 1.9
- norm_shift: float32 [128], replicated, may hold values from -3 to 3
- proj_weight: bfloat16 [128, 512], replicated, may hold values from -0.5 to 0.5
- bias_weight: bfloat16 [128, 4], replicated
- out_weight: bfloat16 [128, 128], replicated, may hold values from -0.5 to 0.5
- token_mask: int32 [1152], replicated, may hold values from 0 to 1, as said below
Outputs:
- update: bfloat16 [1152, 1152, 128], P('row', 'col')
The draws below stay inside these ranges and needn't reach their ends.
Inputs may be any that keep to these rules, and one draw needn't show every extreme that they name: `token_mask`: each of the four aligned quarters of the 1152 tokens is one chain: at least 144 real tokens first, then padding.
All inputs are finite; a program needn't handle non-finite values.
Results may differ from the reference program's by a relative error of at most 0.0075.
The reference program's roundings to bfloat16 on the way count: a program that leaves them out, or rounds other values in their place, can miss the bound.
Values may be sent and summed in bfloat16 or wider, within the bound.
No kernel may reach another device: no remote copies, remote signals or barrier semaphores. Data moves between devices by JAX's collectives and lax.ppermute only.
A program may use at most 192 MiB of HBM per device.

```python
import jax
import jax.numpy as jnp
from jax import lax

C = 128
H = 4
N = 1152


def draw_bias_weight(key, part):
    key = jax.random.fold_in(key, 11)
    factor = 1.0
    base = jax.random.normal(key, (C, H), jnp.float32)
    return (base * (factor / jnp.sqrt(jnp.float32(C)))).astype(jnp.bfloat16)


def draw_token_mask(key, part):
    key = jax.random.fold_in(key, 23)
    quarter = N // 4
    chain_len = jax.random.randint(key, (4,), N // 8, quarter + 1)
    position = jnp.arange(N, dtype=jnp.int32)
    chain_id = position // quarter
    within = position % quarter
    limit = jnp.sum(jnp.where(chain_id[:, None] == jnp.arange(4, dtype=jnp.int32)[None, :], chain_len[None, :], 0), axis=1)
    return (within < limit).astype(jnp.int32)


def steps_of(rng, dims, shards, smallest, high):
    factor_of, own = 1.0, jax.random.fold_in(rng, 6)
    for axis_at, parts in shards:
        steps = jnp.exp(jax.random.uniform(jax.random.fold_in(own, axis_at), (parts,), jnp.float32, smallest / len(shards), high / len(shards)))
        factor_of = factor_of * jnp.repeat(steps, dims[axis_at] // parts).reshape([-1 if axis == axis_at else 1 for axis in range(len(dims))])
    return factor_of


def noise(key, dims, scale, bound, cuts=(), kind=jnp.bfloat16):
    level = steps_of(key, dims, cuts, -0.22, 0.18) if cuts else 1.0
    entries = jax.random.normal(key, dims, jnp.float32) * scale * level
    return jnp.minimum(jnp.maximum(entries, -bound), bound).astype(kind)


def setup_inputs(seed: int = 0) -> dict:
    streams_of = jax.random.split(jax.random.key(seed), 8)
    return {
        "pair_rep": noise(streams_of[0], (N, N, C), 1.0, 6.0, ((0, 16), (1, 8))),
        "norm_gain": jnp.clip(1.0 + 0.18 * jax.random.normal(streams_of[1], (C,), jnp.float32), 0.1, 1.9),
        "norm_shift": noise(streams_of[2], (C,), 0.5, 3.0, (), jnp.float32),
        "proj_weight": noise(streams_of[3], (C, 4 * C), C ** -0.5, 0.5),
        "bias_weight": draw_bias_weight(jax.random.fold_in(streams_of[7], 71), 0),
        "out_weight": noise(streams_of[5], (C, C), C ** -0.5, 0.5),
        "token_mask": draw_token_mask(jax.random.fold_in(streams_of[7], 71), 0),
    }


epsilon = 1e-05

def layer_norm(values, norm_gain, norm_shift):
    wide = values.astype(jnp.float32)
    center = lax.optimization_barrier(jnp.mean(wide, axis=-1, keepdims=True))
    spread = lax.optimization_barrier(jnp.mean((wide - center) ** 2, axis=-1, keepdims=True))
    scaled = (wide - center) / jnp.sqrt(spread + epsilon)
    return (scaled * norm_gain + norm_shift).astype(jnp.bfloat16)

def attend(projected, bias_full, token_mask):
    width = projected.shape[-1] // 4
    heads = bias_full.shape[0]
    rows = projected.shape[0]
    head_size = width // heads
    queries = projected[:, :width].reshape(rows, heads, head_size).astype(jnp.float32)
    key_rows = projected[:, width:2 * width].reshape(rows, heads, head_size).astype(jnp.float32)
    value_rows = projected[:, 2 * width:3 * width].reshape(rows, heads, head_size).astype(jnp.float32)
    gate_part = projected[:, 3 * width:].astype(jnp.float32)
    scores = jnp.einsum('khd,ihd->hki', key_rows, queries) / jnp.sqrt(jnp.float32(head_size))
    scores = scores + bias_full.astype(jnp.float32)
    scores = jnp.where(token_mask[None, :, None] > 0, scores, jnp.float32(-1000000000.0))
    largest = lax.optimization_barrier(jnp.max(scores, axis=1, keepdims=True))
    exps = jnp.exp(scores - largest)
    weights = (exps / lax.optimization_barrier(jnp.sum(exps, axis=1, keepdims=True))).astype(jnp.bfloat16)
    attended = jnp.einsum('hki,khd->ihd', weights.astype(jnp.float32), value_rows).reshape(rows, width)
    return (jax.nn.sigmoid(gate_part) * attended).astype(jnp.bfloat16)

def reference(pair_rep, norm_gain, norm_shift, proj_weight, bias_weight, out_weight, token_mask):
    normed = layer_norm(pair_rep, norm_gain, norm_shift)
    total = normed.shape[0]
    width = normed.shape[2]
    flat_bias = jnp.dot(normed.reshape(total * total, width), bias_weight, preferred_element_type=jnp.float32)
    bias_full = flat_bias.reshape(total, total, -1).transpose(2, 0, 1).astype(jnp.bfloat16)

    def column(index):
        normed_col = lax.dynamic_index_in_dim(normed, index, 1, keepdims=False)
        projected = jnp.dot(normed_col, proj_weight, preferred_element_type=jnp.float32).astype(jnp.bfloat16)
        return attend(projected, bias_full, token_mask)
    gated = lax.map(column, jnp.arange(total, dtype=jnp.int32)).transpose(1, 0, 2)
    update = jnp.dot(gated.reshape(total * total, width), out_weight, preferred_element_type=jnp.float32)
    return update.astype(jnp.bfloat16).reshape(total, total, width)
```

```python
import functools
import math

import jax
import jax.numpy as jnp
from jax import lax
from jax.experimental import pallas as pl
from jax.experimental.pallas import tpu as pltpu
from jax.sharding import PartitionSpec as P

EPSILON = 1e-05
LOG2E = math.log2(math.e)
MASKED = -1e9 * LOG2E
HEADS = 4
MIB = 1024 * 1024

NT = (((1,), (1,)), ((), ()))
TN = (((0,), (0,)), ((), ()))


def dot(a, b, dims=(((1,), (0,)), ((), ()))):
    return lax.dot_general(a, b, dims, preferred_element_type=jnp.float32)


def layer_norm(x, gain, shift):
    x = x.astype(jnp.float32)
    x = x - jnp.mean(x, axis=-1, keepdims=True)
    spread = jnp.mean(x * x, axis=-1, keepdims=True)
    return (x * lax.rsqrt(spread + EPSILON) * gain + shift).astype(jnp.bfloat16)


def bias_kernel(x_ref, gain_ref, shift_ref, bw_ref, bias_ref, main, rest):
    step = pl.program_id(0)
    rows, cols, width = x_ref.shape
    bw = bw_ref[...]

    @pl.when(step == 0)
    def _():
        rest[...] = jnp.zeros_like(rest)

    for r in range(rows):
        normed = layer_norm(x_ref[r], gain_ref[...], shift_ref[...])
        bias = dot(bw, normed, NT)
        at = pl.ds(rows * step + r, 1)
        for h in range(HEADS):
            main[h, at, :] = bias[h : h + 1, :128]
            rest[h, at, 0:16] = bias[h : h + 1, 128:144]

    @pl.when(step == pl.num_programs(0) - 1)
    def _():
        tail = rest[0]
        for h in range(1, HEADS):
            tail = tail + pltpu.roll(rest[h], 16 * h, 1)
        slabs = [main[h].astype(jnp.bfloat16) for h in range(HEADS)]
        slabs.insert(2, tail.astype(jnp.bfloat16))
        for at, slab in enumerate(slabs):
            for copy in range(bias_ref.shape[0]):
                bias_ref[copy, at] = slab


def tile_specs(rows, cols, width):
    return [
        pl.BlockSpec((8, cols, width), lambda s: (s, 0, 0)),
        pl.BlockSpec((1, width), lambda s: (0, 0)),
        pl.BlockSpec((1, width), lambda s: (0, 0)),
    ]


def pair_bias(x, gain, shift, bw, copies):
    rows, cols, width = x.shape
    return pl.pallas_call(
        bias_kernel,
        grid=(rows // 8,),
        in_specs=tile_specs(rows, cols, width) + [pl.BlockSpec((8, width), lambda s: (0, 0))],
        out_specs=pl.BlockSpec((copies, HEADS + 1, rows, 128), lambda s: (0, 0, 0, 0)),
        out_shape=jax.ShapeDtypeStruct((copies, HEADS + 1, rows, 128), jnp.bfloat16),
        scratch_shapes=[
            pltpu.VMEM((HEADS, rows, 128), jnp.float32),
            pltpu.VMEM((HEADS, rows, 128), jnp.float32),
        ],
        compiler_params=pltpu.CompilerParams(vmem_limit_bytes=40 * MIB),
        name="pair_bias",
    )(x, gain, shift, bw)


def norm_kernel(x_ref, gain_ref, shift_ref, normed_ref, wide):
    step = pl.program_id(0)
    rows, cols, width = x_ref.shape
    total = normed_ref.shape[1]
    for r in range(rows):
        normed = layer_norm(x_ref[r], gain_ref[...], shift_ref[...])
        at = pl.multiple_of((rows * step + r) * cols, 8)
        wide[pl.ds(at, cols), :] = normed.astype(jnp.float32)

    @pl.when(step == pl.num_programs(0) - 1)
    def _():
        def col(c, carry):
            normed_ref[c] = wide[pl.ds(c, total, stride=cols), :].astype(jnp.bfloat16)
            return carry

        lax.fori_loop(0, cols, col, 0, unroll=4)


def normed_columns(x, gain, shift):
    rows, cols, width = x.shape
    return pl.pallas_call(
        norm_kernel,
        grid=(rows // 8,),
        in_specs=tile_specs(rows, cols, width),
        out_specs=pl.BlockSpec((cols, rows, width), lambda s: (0, 0, 0)),
        out_shape=jax.ShapeDtypeStruct((cols, rows, width), jnp.bfloat16),
        scratch_shapes=[pltpu.VMEM((rows * cols, width), jnp.float32)],
        compiler_params=pltpu.CompilerParams(vmem_limit_bytes=40 * MIB),
        name="normed_columns",
    )(x, gain, shift)


def place_kernel(*refs):
    parts, o_ref, wide = refs[:-2], refs[-2], refs[-1]
    rows, cols, width = o_ref.shape
    per_group = sum(part.shape[1] for part in parts)

    def group(g, carry):
        at = 0
        for part in parts:
            for c in range(part.shape[1]):
                start = pl.multiple_of((g * per_group + at) * rows, 8)
                wide[pl.ds(start, rows), :] = part[g, c].astype(jnp.float32)
                at += 1
        return carry

    lax.fori_loop(0, cols // per_group, group, 0)

    def row(r, carry):
        o_ref[r] = wide[pl.ds(r, cols, stride=rows), :].astype(jnp.bfloat16)
        return carry

    lax.fori_loop(0, rows, row, 0, unroll=4)


def place(parts, rows, cols, width):
    return pl.pallas_call(
        place_kernel,
        out_shape=jax.ShapeDtypeStruct((rows, cols, width), jnp.bfloat16),
        scratch_shapes=[pltpu.VMEM((rows * cols, width), jnp.float32)],
        compiler_params=pltpu.CompilerParams(vmem_limit_bytes=40 * MIB),
        name="place",
    )(*parts)


GROUPS, TILE, BLOCK = 16, 72, 144
TOKENS = GROUPS * TILE
QUARTERS = 4
QUARTER = TOKENS // QUARTERS
JOBS = 9


def place_of(h, t):
    return (4 * h + t // 2, t % 2) if t < 8 else (JOBS - 1, h)


def attend_kernel(first_head, last, counts_ref, bias_ref, rest_ref, x_ref, *refs):
    if last:
        wqg_ref, wk_ref, wv_ref, wo_ref, earlier_ref, out_ref = refs[:6]
        scratch = refs[6:]
    else:
        wqg_ref, wk_ref, wv_ref, out_ref = refs[:4]
        scratch = refs[4:]
    (bias, top, natural, compact, keys, values_t, q_blocks, gate, attended, exps,
     inverse) = scratch
    step = pl.program_id(0)
    real = [counts_ref[q] for q in range(4)]
    base = [0]
    for q in range(4):
        base.append(base[-1] + counts_ref[4 + q])
    chunks = (base[4] + 127) // 128

    @pl.when(step == 0)
    def _():
        q_blocks[...] = jnp.zeros_like(q_blocks)
        compact[...] = jnp.zeros_like(compact)
        top[...] = jnp.full_like(top, -3e38)

        def fill(job, carry):
            bias[job, QUARTER * 2 :, :] = jnp.full((QUARTER * 2, 256), MASKED, jnp.float32)
            return carry

        lax.fori_loop(0, JOBS, fill, 0)

    @pl.when(step < QUARTERS)
    def _():
        count = real[0]
        start = base[0]
        for q in range(1, QUARTERS):
            count = jnp.where(step == q, real[q], count)
            start = jnp.where(step == q, base[q], start)
        lane = lax.broadcasted_iota(jnp.int32, (TILE, 128), 1)

        for g in range(GROUPS // QUARTERS):
            at = pl.multiple_of(start + TILE * g, 8)
            position = lax.broadcasted_iota(jnp.int32, (TILE, 128), 0) + TILE * g
            keep = position < count

            def put(h, t, value):
                job, half = place_of(h, t)
                value = jnp.where(keep, value * LOG2E, MASKED)
                lanes = slice(128 * half, 128 * half + 128)
                bias[job, pl.ds(at, TILE), lanes] = value
                peak = top[job, :, lanes]
                for s in range(TILE // 8):
                    peak = jnp.maximum(peak, value[8 * s : 8 * s + 8])
                top[job, :, lanes] = peak

            for h in range(2):
                for c in range(8):
                    put(h, c, bias_ref[g, 0, c, h].astype(jnp.float32))
                tail = jnp.zeros((TILE, 128), jnp.float32)
                for c in range(8):
                    part = rest_ref[g, 0, c, 0].astype(jnp.float32)
                    shift = (16 * (c - h - first_head)) % 128
                    if shift:
                        part = pltpu.roll(part, shift, 1)
                    tail = jnp.where(lane // 16 == c, part, tail)
                put(h, 8, tail)

    @pl.when(step == QUARTERS - 1)
    def _():
        def lower(job, carry):
            peak = jnp.max(top[job], axis=0, keepdims=True)
            for s in range(9):
                rows = slice(128 * s, 128 * s + 128)
                bias[job, rows, :] = bias[job, rows, :] - peak
            return carry

        lax.fori_loop(0, JOBS, lower, 0)

    @pl.when(step >= QUARTERS)
    def _():
        for g in range(GROUPS):
            part = x_ref[g, 0].astype(jnp.float32)
            natural[TILE * g : TILE * g + TILE, :] = part
            at = pl.multiple_of(base[g // 4] + TILE * (g % 4), 8)
            compact[pl.ds(at, TILE), :] = part
        x = compact[...].astype(jnp.bfloat16)
        k = dot(x, wk_ref[...]).astype(jnp.bfloat16)
        keys[...] = k
        values_t[...] = dot(wv_ref[...], x, NT).astype(jnp.bfloat16)
        head_of = [lax.broadcasted_iota(jnp.int32, (128, 128), a) // 32 for a in range(2)]
        same_head = (head_of[0] == head_of[1]).astype(jnp.bfloat16)
        k_norm = jnp.max(dot(k * k, same_head))
        q_norm = jnp.float32(0.0)

        scale = jnp.float32(LOG2E / math.sqrt(32.0))
        for t in range(9):
            if t < 8:
                xt = natural[BLOCK * t : BLOCK * t + 128, :]
            else:
                xt = jnp.concatenate(
                    [natural[BLOCK * c + 128 : BLOCK * c + BLOCK, :] for c in range(8)], axis=0
                )
            qg = dot(wqg_ref[...], xt.astype(jnp.bfloat16), NT).astype(jnp.bfloat16)
            qg = qg.astype(jnp.float32)
            gate[:, 128 * t : 128 * t + 128] = 1.0 / (1.0 + jnp.exp(-qg[64:]))
            q = qg[:64] * scale
            high = q.astype(jnp.bfloat16)
            low = (q - high.astype(jnp.float32)).astype(jnp.bfloat16)
            for h in range(2):
                of_head = q[32 * h : 32 * h + 32]
                q_norm = jnp.maximum(
                    q_norm, jnp.max(jnp.sum(of_head * of_head, axis=0, keepdims=True))
                )
                job, half = place_of(h, t)
                lanes = slice(128 * half, 128 * half + 128)
                d = slice(32 * h, 32 * h + 32)
                q_blocks[job, 32 * h : 32 * h + 32, lanes] = high[d]
                q_blocks[job, 64 + 32 * h : 96 + 32 * h, lanes] = low[d]

        small = q_norm * k_norm < 3000.0

        def score_pass(n, safe, job, buf):
            block = q_blocks[job]

            def scores(p):
                rows = slice(*p)
                return dot(keys[rows, :], block) + bias[job, rows, :]

            pieces = [(p, min(p + 256, 128 * n)) for p in range(0, 128 * n, 256)]
            if safe:
                peak = jnp.full((1, 256), -jnp.inf, jnp.float32)
                for p in pieces:
                    peak = jnp.maximum(peak, jnp.max(scores(p), axis=0, keepdims=True))
            total = jnp.zeros((8, 256), jnp.float32)
            for p in pieces:
                e = scores(p)
                if safe:
                    e = e - peak
                e = jnp.exp2(e)
                exps[buf, p[0] : p[1], :] = e
                total = total + jnp.sum(e.reshape((p[1] - p[0]) // 8, 8, 256), axis=0)
            inverse[buf] = jnp.broadcast_to(
                1.0 / jnp.sum(total, axis=0, keepdims=True), (8, 256)
            )

        def value_pass(n, buf):
            scale_by = inverse[buf][0:1]
            total = jnp.zeros((64, 256), jnp.float32)
            for p in range(0, 128 * n, 256):
                rows = slice(p, min(p + 256, 128 * n))
                w = (exps[buf, rows, :] * scale_by).astype(jnp.bfloat16)
                total = total + dot(values_t[:, rows], w)
            return total

        def head_out(n, job, buf):
            total = value_pass(n, buf)
            attended[job] = jnp.where(job >= 4, total[32:], total[:32])

        def run(n, safe):
            score_pass(n, safe, 0, 0)

            def two(i, carry):
                job = 2 * i
                score_pass(n, safe, job + 1, 1)
                head_out(n, job, 0)
                score_pass(n, safe, job + 2, 0)
                head_out(n, job + 1, 1)
                return carry

            lax.fori_loop(0, 4, two, 0)
            total = value_pass(n, 0)
            attended[8] = jnp.concatenate([total[:32, :128], total[32:, 128:]], axis=1)

        for n in range(5, 10):
            pl.when(jnp.logical_and(chunks == n, small))(functools.partial(run, n, False))
        pl.when(jnp.logical_not(small))(functools.partial(run, 9, True))

        for t in range(9):
            tile = slice(128 * t, 128 * t + 128)
            parts = []
            for h in range(2):
                job, half = place_of(h, t)
                parts.append(attended[job, :, 128 * half : 128 * half + 128])
            gated = (gate[:, tile] * jnp.concatenate(parts, axis=0)).astype(jnp.bfloat16)
            if not last:
                out_ref[0, :, tile] = gated
                continue
            gated = jnp.concatenate([earlier_ref[0, :, tile], gated], axis=0)
            update = dot(gated, wo_ref[...], TN)
            if t < 8:
                natural[BLOCK * t : BLOCK * t + 128, :] = update
            else:
                for c in range(8):
                    natural[BLOCK * c + 128 : BLOCK * c + BLOCK, :] = update[16 * c : 16 * c + 16]
        if last:
            for g in range(GROUPS):
                out_ref[g, 0] = natural[TILE * g : TILE * g + TILE, :].astype(jnp.bfloat16)


def attend(first_head, columns, counts, bias, rest, x, weights, earlier=None):
    first, count = columns
    last = earlier is not None
    whole = lambda w: pl.BlockSpec(w.shape, lambda s, counts: (0,) * w.ndim)
    at = lambda s: jnp.maximum(s - QUARTERS, 0)
    quarter = lambda s: jnp.minimum(s, QUARTERS - 1)
    in_specs = [
        pl.BlockSpec(
            (4, 1, 8, 2, TILE, 128),
            lambda s, counts: (quarter(s) % 2, quarter(s) // 2, 0, 0, 0, 0),
        ),
        pl.BlockSpec(
            (4, 1, 8, 1, TILE, 128),
            lambda s, counts: (quarter(s) % 2, quarter(s) // 2, 0, 2, 0, 0),
        ),
        pl.BlockSpec((GROUPS, 1, TILE, 128), lambda s, counts: (0, first + at(s), 0, 0)),
    ] + [whole(w) for w in weights]
    operands = [counts, bias, rest, x, *weights]
    if last:
        in_specs.append(pl.BlockSpec((1, 64, TOKENS), lambda s, counts: (first + at(s), 0, 0)))
        operands.append(earlier)
        out_specs = pl.BlockSpec((GROUPS, 1, TILE, 128), lambda s, counts: (0, at(s), 0, 0))
        out_shape = jax.ShapeDtypeStruct((GROUPS, count, TILE, 128), jnp.bfloat16)
    else:
        out_specs = pl.BlockSpec((1, 64, TOKENS), lambda s, counts: (at(s), 0, 0))
        out_shape = jax.ShapeDtypeStruct((count, 64, TOKENS), jnp.bfloat16)
    return pl.pallas_call(
        functools.partial(attend_kernel, first_head, last),
        grid_spec=pltpu.PrefetchScalarGridSpec(
            num_scalar_prefetch=1,
            grid=(QUARTERS + count,),
            in_specs=in_specs,
            out_specs=out_specs,
            scratch_shapes=[
                pltpu.VMEM((JOBS, TOKENS, 256), jnp.float32),
                pltpu.VMEM((JOBS, 8, 256), jnp.float32),
                pltpu.VMEM((TOKENS, 128), jnp.float32),
                pltpu.VMEM((TOKENS, 128), jnp.float32),
                pltpu.VMEM((TOKENS, 128), jnp.bfloat16),
                pltpu.VMEM((64, TOKENS), jnp.bfloat16),
                pltpu.VMEM((JOBS, 128, 256), jnp.bfloat16),
                pltpu.VMEM((64, TOKENS), jnp.float32),
                pltpu.VMEM((JOBS, 32, 256), jnp.float32),
                pltpu.VMEM((2, TOKENS, 256), jnp.float32),
                pltpu.VMEM((2, 8, 256), jnp.float32),
            ],
        ),
        out_shape=out_shape,
        compiler_params=pltpu.CompilerParams(vmem_limit_bytes=56 * MIB),
        cost_estimate=pl.CostEstimate(
            flops=count * 800_000_000, bytes_accessed=12_000_000, transcendentals=count * 2_400_000
        ),
        name="attend",
    )(*operands)


def head_weights(proj_weight, first_head):
    width = proj_weight.shape[0]
    part = lambda block: proj_weight[
        :, block * width + 32 * first_head : block * width + 32 * first_head + 64
    ]
    wqg = jnp.concatenate([part(0), part(3)], axis=1).T
    wk = jnp.concatenate([part(1), part(1)], axis=1)
    return [wqg, wk, part(2).T]


def key_counts(token_mask, bias_weight):
    real = jnp.sum((token_mask > 0).astype(jnp.int32).reshape(4, QUARTER), axis=1)
    bound = 25.0 * jnp.max(jnp.sum(jnp.abs(bias_weight.astype(jnp.float32)), axis=0))
    kept = jnp.where(bound < 1e8, (real + 7) // 8 * 8, QUARTER)
    return jnp.concatenate([real, kept])


ROW, COL = ("x_hi", "y", "core"), ("z", "x_lo")


def local(pair_rep, norm_gain, norm_shift, proj_weight, bias_weight, out_weight, token_mask):
    rows, cols, width = pair_rep.shape
    per_group = cols // GROUPS
    gain, shift = norm_gain.reshape(1, width), norm_shift.reshape(1, width)
    bw = jnp.pad(bias_weight.T, ((0, 4), (0, 0)))
    bias = pair_bias(pair_rep, gain, shift, bw, 16)
    bias = lax.all_to_all(bias, ("x_hi",) + COL, split_axis=0, concat_axis=0, tiled=True)
    bias = bias.reshape(2, 8, HEADS + 1, rows, 128)
    early = lax.all_gather(bias[:, :, :3], ("y", "core"), axis=0)
    late = lax.all_gather(bias[:, :, 3:], ("y", "core"), axis=0)
    x = normed_columns(pair_rep, gain, shift)
    x = x.reshape(GROUPS, per_group, rows, width)
    x = lax.all_to_all(x, ROW, split_axis=0, concat_axis=0, tiled=True)
    counts = key_counts(token_mask, bias_weight)
    first, second = head_weights(proj_weight, 0), head_weights(proj_weight, 2)
    gated = attend(0, (0, per_group), counts, early, early, x, first)
    update = attend(2, (0, per_group), counts, late, early, x, second + [out_weight], gated)
    update = lax.all_to_all(update, ROW, split_axis=0, concat_axis=0, tiled=True)
    return place([update], rows, cols, width)


def solution(mesh):
    split = jax.sharding.Mesh(mesh.devices.reshape(2, 4, 2, 4, 2), ROW + COL)
    whole = P(ROW, COL, None)
    in_specs = (whole, P(), P(), P(), P(), P(), P())
    return jax.shard_map(local, mesh=split, in_specs=in_specs, out_specs=whole, check_vma=False)
```

```python
import functools
import math

import jax
import jax.numpy as jnp
from jax import lax
from jax.experimental import pallas as pl
from jax.experimental.pallas import tpu as pltpu
from jax.sharding import PartitionSpec as P

EPSILON = 1e-05
LOG2E = math.log2(math.e)
MASKED = -1e9 * LOG2E
HEADS = 4
MIB = 1024 * 1024

NT = (((1,), (1,)), ((), ()))
TN = (((0,), (0,)), ((), ()))


def dot(a, b, dims=(((1,), (0,)), ((), ()))):
    return lax.dot_general(a, b, dims, preferred_element_type=jnp.float32)


def layer_norm(x, gain, shift):
    x = x.astype(jnp.float32)
    x = x - jnp.mean(x, axis=-1, keepdims=True)
    spread = jnp.mean(x * x, axis=-1, keepdims=True)
    return (x * lax.rsqrt(spread + EPSILON) * gain + shift).astype(jnp.bfloat16)


def norm_kernel(x_ref, gain_ref, shift_ref, bw_ref, normed_ref, bias_ref, wide, main, rest):
    step = pl.program_id(0)
    rows, cols, width = x_ref.shape
    total = normed_ref.shape[1]
    bw = bw_ref[...]

    @pl.when(step == 0)
    def _():
        rest[...] = jnp.zeros_like(rest)

    for r in range(rows):
        normed = layer_norm(x_ref[r], gain_ref[...], shift_ref[...])
        at = pl.multiple_of((rows * step + r) * cols, 8)
        wide[pl.ds(at, cols), :] = normed.astype(jnp.float32)
        bias = dot(bw, normed, NT)
        at = pl.ds(rows * step + r, 1)
        for h in range(HEADS):
            main[h, at, :] = bias[h : h + 1, :128]
            rest[h, at, 0:16] = bias[h : h + 1, 128:144]

    @pl.when(step == pl.num_programs(0) - 1)
    def _():
        tail = rest[0]
        for h in range(1, HEADS):
            tail = tail + pltpu.roll(rest[h], 16 * h, 1)
        slabs = [main[h].astype(jnp.bfloat16) for h in range(HEADS)]
        slabs.insert(2, tail.astype(jnp.bfloat16))
        for at, slab in enumerate(slabs):
            for copy in range(bias_ref.shape[0]):
                bias_ref[copy, at] = slab

        def col(c, carry):
            normed_ref[c] = wide[pl.ds(c, total, stride=cols), :].astype(jnp.bfloat16)
            return carry

        lax.fori_loop(0, cols, col, 0, unroll=4)


def norm_and_bias(x, gain, shift, bw, copies):
    rows, cols, width = x.shape
    return pl.pallas_call(
        norm_kernel,
        grid=(rows // 8,),
        in_specs=[
            pl.BlockSpec((8, cols, width), lambda s: (s, 0, 0)),
            pl.BlockSpec((1, width), lambda s: (0, 0)),
            pl.BlockSpec((1, width), lambda s: (0, 0)),
            pl.BlockSpec((8, width), lambda s: (0, 0)),
        ],
        out_specs=[
            pl.BlockSpec((cols, rows, width), lambda s: (0, 0, 0)),
            pl.BlockSpec((copies, HEADS + 1, rows, 128), lambda s: (0, 0, 0, 0)),
        ],
        out_shape=[
            jax.ShapeDtypeStruct((cols, rows, width), jnp.bfloat16),
            jax.ShapeDtypeStruct((copies, HEADS + 1, rows, 128), jnp.bfloat16),
        ],
        scratch_shapes=[
            pltpu.VMEM((rows * cols, width), jnp.float32),
            pltpu.VMEM((HEADS, rows, 128), jnp.float32),
            pltpu.VMEM((HEADS, rows, 128), jnp.float32),
        ],
        compiler_params=pltpu.CompilerParams(vmem_limit_bytes=40 * MIB),
        name="norm_and_bias",
    )(x, gain, shift, bw)


def place_kernel(*refs):
    parts, o_ref, wide = refs[:-2], refs[-2], refs[-1]
    rows, cols, width = o_ref.shape
    per_group = sum(part.shape[1] for part in parts)

    def group(g, carry):
        at = 0
        for part in parts:
            for c in range(part.shape[1]):
                start = pl.multiple_of((g * per_group + at) * rows, 8)
                wide[pl.ds(start, rows), :] = part[g, c].astype(jnp.float32)
                at += 1
        return carry

    lax.fori_loop(0, cols // per_group, group, 0)

    def row(r, carry):
        o_ref[r] = wide[pl.ds(r, cols, stride=rows), :].astype(jnp.bfloat16)
        return carry

    lax.fori_loop(0, rows, row, 0, unroll=4)


def place(parts, rows, cols, width):
    return pl.pallas_call(
        place_kernel,
        out_shape=jax.ShapeDtypeStruct((rows, cols, width), jnp.bfloat16),
        scratch_shapes=[pltpu.VMEM((rows * cols, width), jnp.float32)],
        compiler_params=pltpu.CompilerParams(vmem_limit_bytes=40 * MIB),
        name="place",
    )(*parts)


GROUPS, TILE, BLOCK = 16, 72, 144
TOKENS = GROUPS * TILE
QUARTERS = 4
QUARTER = TOKENS // QUARTERS
JOBS = 9


def place_of(h, t):
    return (4 * h + t // 2, t % 2) if t < 8 else (JOBS - 1, h)


def attend_kernel(first_head, last, counts_ref, bias_ref, rest_ref, x_ref, *refs):
    if last:
        wqg_ref, wk_ref, wv_ref, wo_ref, earlier_ref, out_ref = refs[:6]
        scratch = refs[6:]
    else:
        wqg_ref, wk_ref, wv_ref, out_ref = refs[:4]
        scratch = refs[4:]
    (bias, top, natural, compact, keys, values_t, q_blocks, gate, attended, exps,
     inverse) = scratch
    step = pl.program_id(0)
    real = [counts_ref[q] for q in range(4)]
    base = [0]
    for q in range(4):
        base.append(base[-1] + counts_ref[4 + q])
    chunks = (base[4] + 127) // 128

    @pl.when(step == 0)
    def _():
        q_blocks[...] = jnp.zeros_like(q_blocks)
        compact[...] = jnp.zeros_like(compact)
        top[...] = jnp.full_like(top, -3e38)

        def fill(job, carry):
            bias[job, QUARTER * 2 :, :] = jnp.full((QUARTER * 2, 256), MASKED, jnp.float32)
            return carry

        lax.fori_loop(0, JOBS, fill, 0)

    @pl.when(step < QUARTERS)
    def _():
        count = real[0]
        start = base[0]
        for q in range(1, QUARTERS):
            count = jnp.where(step == q, real[q], count)
            start = jnp.where(step == q, base[q], start)
        lane = lax.broadcasted_iota(jnp.int32, (TILE, 128), 1)

        for g in range(GROUPS // QUARTERS):
            at = pl.multiple_of(start + TILE * g, 8)
            position = lax.broadcasted_iota(jnp.int32, (TILE, 128), 0) + TILE * g
            keep = position < count

            def put(h, t, value):
                job, half = place_of(h, t)
                value = jnp.where(keep, value * LOG2E, MASKED)
                lanes = slice(128 * half, 128 * half + 128)
                bias[job, pl.ds(at, TILE), lanes] = value
                peak = top[job, :, lanes]
                for s in range(TILE // 8):
                    peak = jnp.maximum(peak, value[8 * s : 8 * s + 8])
                top[job, :, lanes] = peak

            for h in range(2):
                for c in range(8):
                    put(h, c, bias_ref[c // 2, g % 2, 0, g // 2, c % 2, h].astype(jnp.float32))
                tail = jnp.zeros((TILE, 128), jnp.float32)
                for c in range(8):
                    part = rest_ref[c // 2, g % 2, 0, g // 2, c % 2, 0].astype(jnp.float32)
                    shift = (16 * (c - h - first_head)) % 128
                    if shift:
                        part = pltpu.roll(part, shift, 1)
                    tail = jnp.where(lane // 16 == c, part, tail)
                put(h, 8, tail)

    @pl.when(step == QUARTERS - 1)
    def _():
        def lower(job, carry):
            peak = jnp.max(top[job], axis=0, keepdims=True)
            for s in range(9):
                rows = slice(128 * s, 128 * s + 128)
                bias[job, rows, :] = bias[job, rows, :] - peak
            return carry

        lax.fori_loop(0, JOBS, lower, 0)

    @pl.when(step >= QUARTERS)
    def _():
        for g in range(GROUPS):
            part = x_ref[g, 0].astype(jnp.float32)
            natural[TILE * g : TILE * g + TILE, :] = part
            at = pl.multiple_of(base[g // 4] + TILE * (g % 4), 8)
            compact[pl.ds(at, TILE), :] = part
        x = compact[...].astype(jnp.bfloat16)
        k = dot(x, wk_ref[...]).astype(jnp.bfloat16)
        keys[...] = k
        values_t[...] = dot(wv_ref[...], x, NT).astype(jnp.bfloat16)
        head_of = [lax.broadcasted_iota(jnp.int32, (128, 128), a) // 32 for a in range(2)]
        same_head = (head_of[0] == head_of[1]).astype(jnp.bfloat16)
        k_norm = jnp.max(dot(k * k, same_head))
        q_norm = jnp.float32(0.0)

        scale = jnp.float32(LOG2E / math.sqrt(32.0))
        for t in range(9):
            if t < 8:
                xt = natural[BLOCK * t : BLOCK * t + 128, :]
            else:
                xt = jnp.concatenate(
                    [natural[BLOCK * c + 128 : BLOCK * c + BLOCK, :] for c in range(8)], axis=0
                )
            qg = dot(wqg_ref[...], xt.astype(jnp.bfloat16), NT).astype(jnp.bfloat16)
            qg = qg.astype(jnp.float32)
            gate[:, 128 * t : 128 * t + 128] = 1.0 / (1.0 + jnp.exp(-qg[64:]))
            q = qg[:64] * scale
            high = q.astype(jnp.bfloat16)
            low = (q - high.astype(jnp.float32)).astype(jnp.bfloat16)
            for h in range(2):
                of_head = q[32 * h : 32 * h + 32]
                q_norm = jnp.maximum(
                    q_norm, jnp.max(jnp.sum(of_head * of_head, axis=0, keepdims=True))
                )
                job, half = place_of(h, t)
                lanes = slice(128 * half, 128 * half + 128)
                d = slice(32 * h, 32 * h + 32)
                q_blocks[job, 32 * h : 32 * h + 32, lanes] = high[d]
                q_blocks[job, 64 + 32 * h : 96 + 32 * h, lanes] = low[d]

        small = q_norm * k_norm < 3000.0

        def score_pass(n, safe, jobs, bufs):
            blocks = [q_blocks[job] for job in jobs]
            pieces = [slice(p, min(p + 512, 128 * n)) for p in range(0, 128 * n, 512)]

            def scores(at, job, rows):
                return dot(keys[rows, :], blocks[at]) + bias[job, rows, :]

            peaks = [jnp.full((1, 256), -jnp.inf, jnp.float32) for _ in jobs]
            if safe:
                for rows in pieces:
                    for at, job in enumerate(jobs):
                        peak = jnp.max(scores(at, job, rows), axis=0, keepdims=True)
                        peaks[at] = jnp.maximum(peaks[at], peak)
            totals = [jnp.zeros((8, 256), jnp.float32) for _ in jobs]
            for rows in pieces:
                for at, job in enumerate(jobs):
                    e = scores(at, job, rows)
                    if safe:
                        e = e - peaks[at]
                    e = jnp.exp2(e)
                    exps[bufs[at], rows, :] = e
                    totals[at] = totals[at] + jnp.sum(e.reshape(-1, 8, 256), axis=0)
            for at, buf in enumerate(bufs):
                total = jnp.sum(totals[at], axis=0, keepdims=True)
                inverse[buf] = jnp.broadcast_to(1.0 / total, (8, 256))

        def value_pass(n, bufs):
            totals = [jnp.zeros((64, 256), jnp.float32) for _ in bufs]
            for p in range(0, 128 * n, 512):
                rows = slice(p, min(p + 512, 128 * n))
                for at, buf in enumerate(bufs):
                    w = (exps[buf, rows, :] * inverse[buf][0:1]).astype(jnp.bfloat16)
                    totals[at] = totals[at] + dot(values_t[:, rows], w)
            return totals

        def mixed(total):
            return jnp.concatenate([total[:32, :128], total[32:, 128:]], axis=1)

        def heads_out(n, jobs, bufs):
            for job, total in zip(jobs, value_pass(n, bufs)):
                if job == JOBS - 1:
                    attended[job] = mixed(total)
                else:
                    attended[job] = total[32:] if job >= 4 else total[:32]

        def run(n):
            groups = [(0, 1, 2), (3, 4, 5), (6, 7, 8)]
            bufs = [(0, 1, 2), (3, 4, 5)]
            score_pass(n, False, groups[0], bufs[0])
            for at in range(3):
                if at < 2:
                    score_pass(n, False, groups[at + 1], bufs[(at + 1) % 2])
                heads_out(n, groups[at], bufs[at % 2])

        def run_safe():
            def one(job, carry):
                score_pass(9, True, (job,), (0,))
                total = value_pass(9, (0,))[0]
                one_head = jnp.where(job >= 4, total[32:], total[:32])
                attended[job] = jnp.where(job == JOBS - 1, mixed(total), one_head)
                return carry

            lax.fori_loop(0, JOBS, one, 0)

        for n in range(5, 10):
            pl.when(jnp.logical_and(chunks == n, small))(functools.partial(run, n))
        pl.when(jnp.logical_not(small))(run_safe)

        for t in range(9):
            tile = slice(128 * t, 128 * t + 128)
            parts = []
            for h in range(2):
                job, half = place_of(h, t)
                parts.append(attended[job, :, 128 * half : 128 * half + 128])
            gated = (gate[:, tile] * jnp.concatenate(parts, axis=0)).astype(jnp.bfloat16)
            if not last:
                out_ref[0, :, tile] = gated
                continue
            gated = jnp.concatenate([earlier_ref[0, :, tile], gated], axis=0)
            update = dot(gated, wo_ref[...], TN)
            if t < 8:
                natural[BLOCK * t : BLOCK * t + 128, :] = update
            else:
                for c in range(8):
                    natural[BLOCK * c + 128 : BLOCK * c + BLOCK, :] = update[16 * c : 16 * c + 16]
        if last:
            for g in range(GROUPS):
                out_ref[g, 0] = natural[TILE * g : TILE * g + TILE, :].astype(jnp.bfloat16)


def attend(first_head, columns, counts, bias, rest, x, weights, earlier=None):
    first, count = columns
    last = earlier is not None
    whole = lambda w: pl.BlockSpec(w.shape, lambda s, counts: (0,) * w.ndim)
    at = lambda s: jnp.maximum(s - QUARTERS, 0)
    quarter = lambda s: jnp.minimum(s, QUARTERS - 1)
    in_specs = [
        pl.BlockSpec(
            (4, 2, 1, 2, 2, 2, TILE, 128),
            lambda s, counts: (0, 0, quarter(s) // 2, quarter(s) % 2, 0, 0, 0, 0),
        ),
        pl.BlockSpec(
            (4, 2, 1, 2, 2, 1, TILE, 128),
            lambda s, counts: (0, 0, quarter(s) // 2, quarter(s) % 2, 0, 2, 0, 0),
        ),
        pl.BlockSpec((GROUPS, 1, TILE, 128), lambda s, counts: (0, first + at(s), 0, 0)),
    ] + [whole(w) for w in weights]
    operands = [counts, bias, rest, x, *weights]
    if last:
        in_specs.append(pl.BlockSpec((1, 64, TOKENS), lambda s, counts: (first + at(s), 0, 0)))
        operands.append(earlier)
        out_specs = pl.BlockSpec((GROUPS, 1, TILE, 128), lambda s, counts: (0, at(s), 0, 0))
        out_shape = jax.ShapeDtypeStruct((GROUPS, count, TILE, 128), jnp.bfloat16)
    else:
        out_specs = pl.BlockSpec((1, 64, TOKENS), lambda s, counts: (at(s), 0, 0))
        out_shape = jax.ShapeDtypeStruct((count, 64, TOKENS), jnp.bfloat16)
    return pl.pallas_call(
        functools.partial(attend_kernel, first_head, last),
        grid_spec=pltpu.PrefetchScalarGridSpec(
            num_scalar_prefetch=1,
            grid=(QUARTERS + count,),
            in_specs=in_specs,
            out_specs=out_specs,
            scratch_shapes=[
                pltpu.VMEM((JOBS, TOKENS, 256), jnp.float32),
                pltpu.VMEM((JOBS, 8, 256), jnp.float32),
                pltpu.VMEM((TOKENS, 128), jnp.float32),
                pltpu.VMEM((TOKENS, 128), jnp.float32),
                pltpu.VMEM((TOKENS, 128), jnp.bfloat16),
                pltpu.VMEM((64, TOKENS), jnp.bfloat16),
                pltpu.VMEM((JOBS, 128, 256), jnp.bfloat16),
                pltpu.VMEM((64, TOKENS), jnp.float32),
                pltpu.VMEM((JOBS, 32, 256), jnp.float32),
                pltpu.VMEM((6, TOKENS, 256), jnp.float32),
                pltpu.VMEM((6, 8, 256), jnp.float32),
            ],
        ),
        out_shape=out_shape,
        compiler_params=pltpu.CompilerParams(vmem_limit_bytes=56 * MIB),
        cost_estimate=pl.CostEstimate(
            flops=count * 800_000_000, bytes_accessed=12_000_000, transcendentals=count * 2_400_000
        ),
        name="attend",
    )(*operands)


def head_weights(proj_weight, first_head):
    width = proj_weight.shape[0]
    part = lambda block: proj_weight[
        :, block * width + 32 * first_head : block * width + 32 * first_head + 64
    ]
    wqg = jnp.concatenate([part(0), part(3)], axis=1).T
    wk = jnp.concatenate([part(1), part(1)], axis=1)
    return [wqg, wk, part(2).T]


def key_counts(token_mask, bias_weight):
    real = jnp.sum((token_mask > 0).astype(jnp.int32).reshape(4, QUARTER), axis=1)
    bound = 25.0 * jnp.max(jnp.sum(jnp.abs(bias_weight.astype(jnp.float32)), axis=0))
    kept = jnp.where(bound < 1e8, (real + 7) // 8 * 8, QUARTER)
    return jnp.concatenate([real, kept])


ROW, COL = ("x_hi", "y", "core"), ("z", "x_lo")


def local(pair_rep, norm_gain, norm_shift, proj_weight, bias_weight, out_weight, token_mask):
    rows, cols, width = pair_rep.shape
    per_group = cols // GROUPS
    gain, shift = norm_gain.reshape(1, width), norm_shift.reshape(1, width)
    bw = jnp.pad(bias_weight.T, ((0, 4), (0, 0)))
    x, bias = norm_and_bias(pair_rep, gain, shift, bw, 16)
    x = x.reshape(GROUPS, per_group, rows, width)
    x = lax.all_to_all(x, ROW, split_axis=0, concat_axis=0, tiled=True)
    bias = lax.all_to_all(bias, ("x_hi", "y", "x_lo"), split_axis=0, concat_axis=0, tiled=True)

    def gather(part):
        part = lax.all_gather(part, ("z", "core"), axis=0)
        return part.reshape(4, 2, 2, 4, 2, -1, rows, 128)

    early, late = gather(bias[:, :3]), gather(bias[:, 3:])
    counts = key_counts(token_mask, bias_weight)
    first, second = head_weights(proj_weight, 0), head_weights(proj_weight, 2)
    gated = attend(0, (0, per_group), counts, early, early, x, first)
    update = attend(2, (0, per_group), counts, late, early, x, second + [out_weight], gated)
    update = lax.all_to_all(update, ROW, split_axis=0, concat_axis=0, tiled=True)
    return place([update], rows, cols, width)


def solution(mesh):
    split = jax.sharding.Mesh(mesh.devices.reshape(2, 4, 2, 4, 2), ROW + COL)
    whole = P(ROW, COL, None)
    in_specs = (whole, P(), P(), P(), P(), P(), P())
    return jax.shard_map(local, mesh=split, in_specs=in_specs, out_specs=whole, check_vma=False)
```

```python
import functools
import math

import jax
import jax.numpy as jnp
from jax import lax
from jax.experimental import pallas as pl
from jax.experimental.pallas import tpu as pltpu
from jax.sharding import PartitionSpec as P

EPSILON = 1e-05
LOG2E = math.log2(math.e)
MASKED = -1e9 * LOG2E
HEADS = 4
MIB = 1024 * 1024

NT = (((1,), (1,)), ((), ()))
TN = (((0,), (0,)), ((), ()))


def dot(a, b, dims=(((1,), (0,)), ((), ()))):
    return lax.dot_general(a, b, dims, preferred_element_type=jnp.float32)


def layer_norm(x, gain, shift):
    x = x.astype(jnp.float32)
    x = x - jnp.mean(x, axis=-1, keepdims=True)
    spread = jnp.mean(x * x, axis=-1, keepdims=True)
    return (x * lax.rsqrt(spread + EPSILON) * gain + shift).astype(jnp.bfloat16)


def norm_kernel(x_ref, params_ref, normed_ref, bias_ref, wide, main, rest):
    step = pl.program_id(0)
    rows, cols, width = x_ref.shape
    total = normed_ref.shape[1]
    gain, shift = params_ref[8:9], params_ref[9:10]
    bw = params_ref[0:8].astype(jnp.bfloat16)

    @pl.when(step == 0)
    def _():
        rest[...] = jnp.zeros_like(rest)

    for r in range(rows):
        normed = layer_norm(x_ref[r], gain, shift)
        at = pl.multiple_of((rows * step + r) * cols, 8)
        wide[pl.ds(at, cols), :] = normed.astype(jnp.float32)
        bias = dot(bw, normed, NT)
        at = pl.ds(rows * step + r, 1)
        for h in range(HEADS):
            main[h, at, :] = bias[h : h + 1, :128]
            rest[h, at, 0:16] = bias[h : h + 1, 128:144]

    @pl.when(step == pl.num_programs(0) - 1)
    def _():
        tail = rest[0]
        for h in range(1, HEADS):
            tail = tail + pltpu.roll(rest[h], 16 * h, 1)
        slabs = [main[h].astype(jnp.bfloat16) for h in range(HEADS)]
        slabs.insert(2, tail.astype(jnp.bfloat16))
        for at, slab in enumerate(slabs):
            for copy in range(bias_ref.shape[0]):
                bias_ref[copy, at] = slab

        def col(c, carry):
            normed_ref[c] = wide[pl.ds(c, total, stride=cols), :].astype(jnp.bfloat16)
            return carry

        lax.fori_loop(0, cols, col, 0, unroll=4)


def norm_and_bias(x, params, copies):
    rows, cols, width = x.shape
    return pl.pallas_call(
        norm_kernel,
        grid=(rows // 8,),
        in_specs=[
            pl.BlockSpec((8, cols, width), lambda s: (s, 0, 0)),
            pl.BlockSpec((16, width), lambda s: (0, 0)),
        ],
        out_specs=[
            pl.BlockSpec((cols, rows, width), lambda s: (0, 0, 0)),
            pl.BlockSpec((copies, HEADS + 1, rows, 128), lambda s: (0, 0, 0, 0)),
        ],
        out_shape=[
            jax.ShapeDtypeStruct((cols, rows, width), jnp.bfloat16),
            jax.ShapeDtypeStruct((copies, HEADS + 1, rows, 128), jnp.bfloat16),
        ],
        scratch_shapes=[
            pltpu.VMEM((rows * cols, width), jnp.float32),
            pltpu.VMEM((HEADS, rows, 128), jnp.float32),
            pltpu.VMEM((HEADS, rows, 128), jnp.float32),
        ],
        compiler_params=pltpu.CompilerParams(vmem_limit_bytes=40 * MIB),
        name="norm_and_bias",
    )(x, params)


def place_kernel(*refs):
    parts, o_ref, wide = refs[:-2], refs[-2], refs[-1]
    rows, cols, width = o_ref.shape
    per_group = sum(part.shape[1] for part in parts)

    def group(g, carry):
        at = 0
        for part in parts:
            for c in range(part.shape[1]):
                start = pl.multiple_of((g * per_group + at) * rows, 8)
                wide[pl.ds(start, rows), :] = part[g, c].astype(jnp.float32)
                at += 1
        return carry

    lax.fori_loop(0, cols // per_group, group, 0)

    def row(r, carry):
        o_ref[r] = wide[pl.ds(r, cols, stride=rows), :].astype(jnp.bfloat16)
        return carry

    lax.fori_loop(0, rows, row, 0, unroll=4)


def place(parts, rows, cols, width):
    return pl.pallas_call(
        place_kernel,
        out_shape=jax.ShapeDtypeStruct((rows, cols, width), jnp.bfloat16),
        scratch_shapes=[pltpu.VMEM((rows * cols, width), jnp.float32)],
        compiler_params=pltpu.CompilerParams(vmem_limit_bytes=40 * MIB),
        name="place",
    )(*parts)


GROUPS, TILE, BLOCK = 16, 72, 144
TOKENS = GROUPS * TILE
QUARTERS = 4
QUARTER = TOKENS // QUARTERS
JOBS = 9


def place_of(h, t):
    return (4 * h + t // 2, t % 2) if t < 8 else (JOBS - 1, h)


def attend_kernel(first_head, last, counts_ref, bias_ref, rest_ref, x_ref, *refs):
    if last:
        wqg_ref, wk_ref, wv_ref, wo_ref, earlier_ref, out_ref = refs[:6]
        scratch = refs[6:]
    else:
        wqg_ref, wk_ref, wv_ref, out_ref = refs[:4]
        scratch = refs[4:]
    (bias, top, natural, compact, keys, values_t, q_blocks, gate, attended, exps,
     inverse, next_values, next_gate, result, small_ref) = scratch
    step = pl.program_id(0)
    real = [counts_ref[q] for q in range(4)]
    base = [0]
    for q in range(4):
        base.append(base[-1] + counts_ref[4 + q])
    chunks = (base[4] + 127) // 128

    @pl.when(step == 0)
    def _():
        q_blocks[...] = jnp.zeros_like(q_blocks)
        compact[...] = jnp.zeros_like(compact)
        top[...] = jnp.full_like(top, -3e38)

        def fill(job, carry):
            bias[job, QUARTER * 2 :, :] = jnp.full((QUARTER * 2, 256), MASKED, jnp.float32)
            return carry

        lax.fori_loop(0, JOBS, fill, 0)

    @pl.when(step < QUARTERS)
    def _():
        count = real[0]
        start = base[0]
        for q in range(1, QUARTERS):
            count = jnp.where(step == q, real[q], count)
            start = jnp.where(step == q, base[q], start)
        lane = lax.broadcasted_iota(jnp.int32, (TILE, 128), 1)

        for g in range(GROUPS // QUARTERS):
            at = pl.multiple_of(start + TILE * g, 8)
            position = lax.broadcasted_iota(jnp.int32, (TILE, 128), 0) + TILE * g
            keep = position < count

            def put(h, t, value):
                job, half = place_of(h, t)
                value = jnp.where(keep, value * LOG2E, MASKED)
                lanes = slice(128 * half, 128 * half + 128)
                bias[job, pl.ds(at, TILE), lanes] = value
                peak = top[job, :, lanes]
                for s in range(TILE // 8):
                    peak = jnp.maximum(peak, value[8 * s : 8 * s + 8])
                top[job, :, lanes] = peak

            for h in range(2):
                for c in range(8):
                    put(h, c, bias_ref[c // 2, g % 2, 0, g // 2, c % 2, h].astype(jnp.float32))
                tail = jnp.zeros((TILE, 128), jnp.float32)
                for c in range(8):
                    part = rest_ref[c // 2, g % 2, 0, g // 2, c % 2, 0].astype(jnp.float32)
                    shift = (16 * (c - h - first_head)) % 128
                    if shift:
                        part = pltpu.roll(part, shift, 1)
                    tail = jnp.where(lane // 16 == c, part, tail)
                put(h, 8, tail)

    @pl.when(step == QUARTERS - 1)
    def _():
        def lower(job, carry):
            peak = jnp.max(top[job], axis=0, keepdims=True)
            for s in range(9):
                rows = slice(128 * s, 128 * s + 128)
                bias[job, rows, :] = bias[job, rows, :] - peak
            return carry

        lax.fori_loop(0, JOBS, lower, 0)

    def prepare():
        for g in range(GROUPS):
            part = x_ref[g, 0].astype(jnp.float32)
            natural[TILE * g : TILE * g + TILE, :] = part
            at = pl.multiple_of(base[g // 4] + TILE * (g % 4), 8)
            compact[pl.ds(at, TILE), :] = part
        x = compact[...].astype(jnp.bfloat16)
        k = dot(x, wk_ref[...]).astype(jnp.bfloat16)
        keys[...] = k
        next_values[...] = dot(wv_ref[...], x, NT).astype(jnp.bfloat16)
        head_of = [lax.broadcasted_iota(jnp.int32, (128, 128), a) // 32 for a in range(2)]
        same_head = (head_of[0] == head_of[1]).astype(jnp.bfloat16)
        k_norm = jnp.max(dot(k * k, same_head))
        q_norm = jnp.float32(0.0)

        scale = jnp.float32(LOG2E / math.sqrt(32.0))
        for t in range(9):
            if t < 8:
                xt = natural[BLOCK * t : BLOCK * t + 128, :]
            else:
                xt = jnp.concatenate(
                    [natural[BLOCK * c + 128 : BLOCK * c + BLOCK, :] for c in range(8)], axis=0
                )
            qg = dot(wqg_ref[...], xt.astype(jnp.bfloat16), NT).astype(jnp.bfloat16)
            qg = qg.astype(jnp.float32)
            next_gate[:, 128 * t : 128 * t + 128] = 1.0 / (1.0 + jnp.exp(-qg[64:]))
            q = qg[:64] * scale
            high = q.astype(jnp.bfloat16)
            low = (q - high.astype(jnp.float32)).astype(jnp.bfloat16)
            for h in range(2):
                of_head = q[32 * h : 32 * h + 32]
                q_norm = jnp.maximum(
                    q_norm, jnp.max(jnp.sum(of_head * of_head, axis=0, keepdims=True))
                )
                job, half = place_of(h, t)
                lanes = slice(128 * half, 128 * half + 128)
                d = slice(32 * h, 32 * h + 32)
                q_blocks[job, 32 * h : 32 * h + 32, lanes] = high[d]
                q_blocks[job, 64 + 32 * h : 96 + 32 * h, lanes] = low[d]
        small_ref[0] = (q_norm * k_norm < 3000.0).astype(jnp.int32)

    @pl.when(step == QUARTERS - 1)
    def _():
        prepare()

    @pl.when(step >= QUARTERS)
    def _():
        small = small_ref[0] > 0
        values_t[...] = next_values[...]
        gate[...] = next_gate[...]

        def score_pass(n, safe, jobs, bufs):
            blocks = [q_blocks[job] for job in jobs]
            pieces = [slice(p, min(p + 512, 128 * n)) for p in range(0, 128 * n, 512)]

            def scores(at, job, rows):
                return dot(keys[rows, :], blocks[at]) + bias[job, rows, :]

            peaks = [jnp.full((1, 256), -jnp.inf, jnp.float32) for _ in jobs]
            if safe:
                for rows in pieces:
                    for at, job in enumerate(jobs):
                        peak = jnp.max(scores(at, job, rows), axis=0, keepdims=True)
                        peaks[at] = jnp.maximum(peaks[at], peak)
            totals = [jnp.zeros((8, 256), jnp.float32) for _ in jobs]
            for rows in pieces:
                for at, job in enumerate(jobs):
                    e = scores(at, job, rows)
                    if safe:
                        e = e - peaks[at]
                    e = jnp.exp2(e)
                    exps[bufs[at], rows, :] = e
                    totals[at] = totals[at] + jnp.sum(e.reshape(-1, 8, 256), axis=0)
            for at, buf in enumerate(bufs):
                total = jnp.sum(totals[at], axis=0, keepdims=True)
                inverse[buf] = jnp.broadcast_to(1.0 / total, (8, 256))

        def value_pass(n, bufs):
            totals = [jnp.zeros((64, 256), jnp.float32) for _ in bufs]
            for p in range(0, 128 * n, 512):
                rows = slice(p, min(p + 512, 128 * n))
                for at, buf in enumerate(bufs):
                    w = (exps[buf, rows, :] * inverse[buf][0:1]).astype(jnp.bfloat16)
                    totals[at] = totals[at] + dot(values_t[:, rows], w)
            return totals

        def mixed(total):
            return jnp.concatenate([total[:32, :128], total[32:, 128:]], axis=1)

        def heads_out(n, jobs, bufs):
            for job, total in zip(jobs, value_pass(n, bufs)):
                if job == JOBS - 1:
                    attended[job] = mixed(total)
                else:
                    attended[job] = total[32:] if job >= 4 else total[:32]

        def finish():
            for t in range(9):
                tile = slice(128 * t, 128 * t + 128)
                parts = []
                for h in range(2):
                    job, half = place_of(h, t)
                    parts.append(attended[job, :, 128 * half : 128 * half + 128])
                gated = (gate[:, tile] * jnp.concatenate(parts, axis=0)).astype(jnp.bfloat16)
                if not last:
                    out_ref[0, :, tile] = gated
                    continue
                gated = jnp.concatenate([earlier_ref[0, :, tile], gated], axis=0)
                update = dot(gated, wo_ref[...], TN)
                if t < 8:
                    result[BLOCK * t : BLOCK * t + 128, :] = update
                else:
                    for c in range(8):
                        result[BLOCK * c + 128 : BLOCK * c + BLOCK, :] = update[16 * c : 16 * c + 16]
            if last:
                for g in range(GROUPS):
                    out_ref[g, 0] = result[TILE * g : TILE * g + TILE, :].astype(jnp.bfloat16)

        def run(n):
            score_pass(n, False, (0, 1, 2), (0, 1, 2))
            score_pass(n, False, (3, 4, 5), (3, 4, 5))
            heads_out(n, (0, 1, 2), (0, 1, 2))
            score_pass(n, False, (6, 7, 8), (0, 1, 2))
            prepare()
            heads_out(n, (3, 4, 5), (3, 4, 5))
            heads_out(n, (6, 7, 8), (0, 1, 2))
            finish()

        def run_safe():
            def one(job, carry):
                score_pass(9, True, (job,), (0,))
                total = value_pass(9, (0,))[0]
                one_head = jnp.where(job >= 4, total[32:], total[:32])
                attended[job] = jnp.where(job == JOBS - 1, mixed(total), one_head)
                return carry

            lax.fori_loop(0, JOBS, one, 0)
            prepare()
            finish()

        for n in range(5, 10):
            pl.when(jnp.logical_and(chunks == n, small))(functools.partial(run, n))
        pl.when(jnp.logical_not(small))(run_safe)


def attend(first_head, columns, counts, bias, rest, x, weights, earlier=None):
    first, count = columns
    last = earlier is not None
    whole = lambda w: pl.BlockSpec(w.shape, lambda s, counts: (0,) * w.ndim)
    at = lambda s: jnp.maximum(s - QUARTERS, 0)
    ahead = lambda s: jnp.clip(s - QUARTERS + 1, 0, count - 1)
    quarter = lambda s: jnp.minimum(s, QUARTERS - 1)
    in_specs = [
        pl.BlockSpec(
            (4, 2, 1, 2, 2, 2, TILE, 128),
            lambda s, counts: (0, 0, quarter(s) // 2, quarter(s) % 2, 0, 0, 0, 0),
        ),
        pl.BlockSpec(
            (4, 2, 1, 2, 2, 1, TILE, 128),
            lambda s, counts: (0, 0, quarter(s) // 2, quarter(s) % 2, 0, 2, 0, 0),
        ),
        pl.BlockSpec((GROUPS, 1, TILE, 128), lambda s, counts: (0, first + ahead(s), 0, 0)),
    ] + [whole(w) for w in weights]
    operands = [counts, bias, rest, x, *weights]
    if last:
        in_specs.append(pl.BlockSpec((1, 64, TOKENS), lambda s, counts: (first + at(s), 0, 0)))
        operands.append(earlier)
        out_specs = pl.BlockSpec((GROUPS, 1, TILE, 128), lambda s, counts: (0, at(s), 0, 0))
        out_shape = jax.ShapeDtypeStruct((GROUPS, count, TILE, 128), jnp.bfloat16)
    else:
        out_specs = pl.BlockSpec((1, 64, TOKENS), lambda s, counts: (at(s), 0, 0))
        out_shape = jax.ShapeDtypeStruct((count, 64, TOKENS), jnp.bfloat16)
    return pl.pallas_call(
        functools.partial(attend_kernel, first_head, last),
        grid_spec=pltpu.PrefetchScalarGridSpec(
            num_scalar_prefetch=1,
            grid=(QUARTERS + count,),
            in_specs=in_specs,
            out_specs=out_specs,
            scratch_shapes=[
                pltpu.VMEM((JOBS, TOKENS, 256), jnp.float32),
                pltpu.VMEM((JOBS, 8, 256), jnp.float32),
                pltpu.VMEM((TOKENS, 128), jnp.float32),
                pltpu.VMEM((TOKENS, 128), jnp.float32),
                pltpu.VMEM((TOKENS, 128), jnp.bfloat16),
                pltpu.VMEM((64, TOKENS), jnp.bfloat16),
                pltpu.VMEM((JOBS, 128, 256), jnp.bfloat16),
                pltpu.VMEM((64, TOKENS), jnp.float32),
                pltpu.VMEM((JOBS, 32, 256), jnp.float32),
                pltpu.VMEM((6, TOKENS, 256), jnp.float32),
                pltpu.VMEM((6, 8, 256), jnp.float32),
                pltpu.VMEM((64, TOKENS), jnp.bfloat16),
                pltpu.VMEM((64, TOKENS), jnp.float32),
                pltpu.VMEM((TOKENS, 128), jnp.float32),
                pltpu.SMEM((1,), jnp.int32),
            ],
        ),
        out_shape=out_shape,
        compiler_params=pltpu.CompilerParams(vmem_limit_bytes=56 * MIB),
        cost_estimate=pl.CostEstimate(
            flops=count * 800_000_000, bytes_accessed=12_000_000, transcendentals=count * 2_400_000
        ),
        name="attend",
    )(*operands)


def head_weights(proj_weight, first_head):
    width = proj_weight.shape[0]
    part = lambda block: proj_weight[
        :, block * width + 32 * first_head : block * width + 32 * first_head + 64
    ]
    wqg = jnp.concatenate([part(0), part(3)], axis=1).T
    wk = jnp.concatenate([part(1), part(1)], axis=1)
    return [wqg, wk, part(2).T]


def key_counts(token_mask, bias_weight):
    real = jnp.sum((token_mask > 0).astype(jnp.int32).reshape(4, QUARTER), axis=1)
    bound = 25.0 * jnp.max(jnp.sum(jnp.abs(bias_weight.astype(jnp.float32)), axis=0))
    kept = jnp.where(bound < 1e8, (real + 7) // 8 * 8, QUARTER)
    return jnp.concatenate([real, kept])


ROW, COL = ("x_hi", "y", "core"), ("z", "x_lo")


def local(pair_rep, norm_gain, norm_shift, proj_weight, bias_weight, out_weight, token_mask):
    rows, cols, width = pair_rep.shape
    per_group = cols // GROUPS
    params = jnp.concatenate(
        [bias_weight.T.astype(jnp.float32), jnp.zeros((4, width), jnp.float32),
         norm_gain[None], norm_shift[None], jnp.zeros((6, width), jnp.float32)], axis=0
    )
    x, bias = norm_and_bias(pair_rep, params, 16)
    x = x.reshape(GROUPS, per_group, rows, width)
    x = lax.all_to_all(x, ROW, split_axis=0, concat_axis=0, tiled=True)
    bias = lax.all_to_all(bias, ("x_hi", "y", "x_lo"), split_axis=0, concat_axis=0, tiled=True)

    def gather(part):
        part = lax.all_gather(part, ("z", "core"), axis=0)
        return part.reshape(4, 2, 2, 4, 2, -1, rows, 128)

    early, late = gather(bias[:, :3]), gather(bias[:, 3:])
    counts = key_counts(token_mask, bias_weight)
    first, second = head_weights(proj_weight, 0), head_weights(proj_weight, 2)
    gated = attend(0, (0, per_group), counts, early, early, x, first)
    update = attend(2, (0, per_group), counts, late, early, x, second + [out_weight], gated)
    update = lax.all_to_all(update, ROW, split_axis=0, concat_axis=0, tiled=True)
    return place([update], rows, cols, width)


def solution(mesh):
    split = jax.sharding.Mesh(mesh.devices.reshape(2, 4, 2, 4, 2), ROW + COL)
    whole = P(ROW, COL, None)
    in_specs = (whole, P(), P(), P(), P(), P(), P())
    return jax.shard_map(local, mesh=split, in_specs=in_specs, out_specs=whole, check_vma=False)
```

```python
import functools
import math

import jax
import jax.numpy as jnp
from jax import lax
from jax.experimental import pallas as pl
from jax.experimental.pallas import tpu as pltpu
from jax.sharding import PartitionSpec as P

EPSILON = 1e-05
LOG2E = math.log2(math.e)
MASKED = -1e9 * LOG2E
HEADS = 4
MIB = 1024 * 1024

NT = (((1,), (1,)), ((), ()))
TN = (((0,), (0,)), ((), ()))


def dot(a, b, dims=(((1,), (0,)), ((), ()))):
    return lax.dot_general(a, b, dims, preferred_element_type=jnp.float32)


def layer_norm(x, gain, shift):
    x = x.astype(jnp.float32)
    x = x - jnp.mean(x, axis=-1, keepdims=True)
    spread = jnp.mean(x * x, axis=-1, keepdims=True)
    return (x * lax.rsqrt(spread + EPSILON) * gain + shift).astype(jnp.bfloat16)


def norm_kernel(x_ref, params_ref, normed_ref, bias_ref, wide, main, rest):
    step = pl.program_id(0)
    rows, cols, width = x_ref.shape
    total = normed_ref.shape[1]
    gain, shift = params_ref[8:9], params_ref[9:10]
    bw = params_ref[0:8].astype(jnp.bfloat16)

    @pl.when(step == 0)
    def _():
        rest[...] = jnp.zeros_like(rest)

    for r in range(rows):
        normed = layer_norm(x_ref[r], gain, shift)
        at = pl.multiple_of((rows * step + r) * cols, 8)
        wide[pl.ds(at, cols), :] = normed.astype(jnp.float32)
        bias = dot(bw, normed, NT)
        at = pl.ds(rows * step + r, 1)
        for h in range(HEADS):
            main[h, at, :] = bias[h : h + 1, :128]
            rest[h, at, 0:16] = bias[h : h + 1, 128:144]

    @pl.when(step == pl.num_programs(0) - 1)
    def _():
        tail = rest[0]
        for h in range(1, HEADS):
            tail = tail + pltpu.roll(rest[h], 16 * h, 1)
        slabs = [main[h].astype(jnp.bfloat16) for h in range(HEADS)]
        slabs.insert(2, tail.astype(jnp.bfloat16))
        for at, slab in enumerate(slabs):
            for copy in range(bias_ref.shape[0]):
                bias_ref[copy, at] = slab

        def col(c, carry):
            normed_ref[c] = wide[pl.ds(c, total, stride=cols), :].astype(jnp.bfloat16)
            return carry

        lax.fori_loop(0, cols, col, 0, unroll=4)


def norm_and_bias(x, params, copies):
    rows, cols, width = x.shape
    return pl.pallas_call(
        norm_kernel,
        grid=(rows // 8,),
        in_specs=[
            pl.BlockSpec((8, cols, width), lambda s: (s, 0, 0)),
            pl.BlockSpec((16, width), lambda s: (0, 0)),
        ],
        out_specs=[
            pl.BlockSpec((cols, rows, width), lambda s: (0, 0, 0)),
            pl.BlockSpec((copies, HEADS + 1, rows, 128), lambda s: (0, 0, 0, 0)),
        ],
        out_shape=[
            jax.ShapeDtypeStruct((cols, rows, width), jnp.bfloat16),
            jax.ShapeDtypeStruct((copies, HEADS + 1, rows, 128), jnp.bfloat16),
        ],
        scratch_shapes=[
            pltpu.VMEM((rows * cols, width), jnp.float32),
            pltpu.VMEM((HEADS, rows, 128), jnp.float32),
            pltpu.VMEM((HEADS, rows, 128), jnp.float32),
        ],
        compiler_params=pltpu.CompilerParams(vmem_limit_bytes=40 * MIB),
        name="norm_and_bias",
    )(x, params)


def place_kernel(*refs):
    parts, o_ref, wide = refs[:-2], refs[-2], refs[-1]
    rows, cols, width = o_ref.shape
    per_group = sum(part.shape[1] for part in parts)

    def group(g, carry):
        at = 0
        for part in parts:
            for c in range(part.shape[1]):
                start = pl.multiple_of((g * per_group + at) * rows, 8)
                wide[pl.ds(start, rows), :] = part[g, c].astype(jnp.float32)
                at += 1
        return carry

    lax.fori_loop(0, cols // per_group, group, 0)

    def row(r, carry):
        o_ref[r] = wide[pl.ds(r, cols, stride=rows), :].astype(jnp.bfloat16)
        return carry

    lax.fori_loop(0, rows, row, 0, unroll=4)


def place(parts, rows, cols, width):
    return pl.pallas_call(
        place_kernel,
        out_shape=jax.ShapeDtypeStruct((rows, cols, width), jnp.bfloat16),
        scratch_shapes=[pltpu.VMEM((rows * cols, width), jnp.float32)],
        compiler_params=pltpu.CompilerParams(vmem_limit_bytes=40 * MIB),
        name="place",
    )(*parts)


GROUPS, TILE, BLOCK = 16, 72, 144
TOKENS = GROUPS * TILE
QUARTERS = 4
QUARTER = TOKENS // QUARTERS
JOBS = 9


def place_of(h, t):
    return (4 * h + t // 2, t % 2) if t < 8 else (JOBS - 1, h)


def attend_kernel(first_head, last, counts_ref, bias_ref, rest_ref, x_ref, *refs):
    if last:
        wqg_ref, wk_ref, wv_ref, wo_ref, earlier_ref, out_ref = refs[:6]
        scratch = refs[6:]
    else:
        wqg_ref, wk_ref, wv_ref, out_ref = refs[:4]
        scratch = refs[4:]
    (bias, top, natural, compact, keys, values_t, q_blocks, gate, attended, exps,
     inverse, next_values, next_gate, result, small_ref) = scratch
    step = pl.program_id(0)
    real = [counts_ref[q] for q in range(4)]
    base = [0]
    for q in range(4):
        base.append(base[-1] + counts_ref[4 + q])
    chunks = (base[4] + 127) // 128

    @pl.when(step == 0)
    def _():
        q_blocks[...] = jnp.zeros_like(q_blocks)
        compact[...] = jnp.zeros_like(compact)
        top[...] = jnp.full_like(top, -3e38)

        def fill(job, carry):
            bias[job, QUARTER * 2 :, :] = jnp.full((QUARTER * 2, 256), MASKED, jnp.float32)
            return carry

        lax.fori_loop(0, JOBS, fill, 0)

    @pl.when(step < QUARTERS)
    def _():
        count = real[0]
        start = base[0]
        for q in range(1, QUARTERS):
            count = jnp.where(step == q, real[q], count)
            start = jnp.where(step == q, base[q], start)
        lane = lax.broadcasted_iota(jnp.int32, (TILE, 128), 1)

        for g in range(GROUPS // QUARTERS):
            at = pl.multiple_of(start + TILE * g, 8)
            position = lax.broadcasted_iota(jnp.int32, (TILE, 128), 0) + TILE * g
            keep = position < count

            def put(h, t, value):
                job, half = place_of(h, t)
                value = jnp.where(keep, value * LOG2E, MASKED)
                lanes = slice(128 * half, 128 * half + 128)
                bias[job, pl.ds(at, TILE), lanes] = value
                peak = top[job, :, lanes]
                for s in range(TILE // 8):
                    peak = jnp.maximum(peak, value[8 * s : 8 * s + 8])
                top[job, :, lanes] = peak

            for h in range(2):
                for c in range(8):
                    put(h, c, bias_ref[c // 2, g % 2, 0, g // 2, c % 2, h].astype(jnp.float32))
                tail = jnp.zeros((TILE, 128), jnp.float32)
                for c in range(8):
                    part = rest_ref[c // 2, g % 2, 0, g // 2, c % 2, 0].astype(jnp.float32)
                    shift = (16 * (c - h - first_head)) % 128
                    if shift:
                        part = pltpu.roll(part, shift, 1)
                    tail = jnp.where(lane // 16 == c, part, tail)
                put(h, 8, tail)

    @pl.when(step == QUARTERS - 1)
    def _():
        peaks = jnp.max(top[...], axis=1)

        @pl.when(jnp.max(jnp.abs(peaks)) >= 30.0)
        def _():
            def lower(job, carry):
                peak = jnp.max(top[job], axis=0, keepdims=True)
                for s in range(9):
                    rows = slice(128 * s, 128 * s + 128)
                    bias[job, rows, :] = bias[job, rows, :] - peak
                return carry

            lax.fori_loop(0, JOBS, lower, 0)

    def prepare():
        for g in range(GROUPS):
            part = x_ref[g, 0].astype(jnp.float32)
            natural[TILE * g : TILE * g + TILE, :] = part
            at = pl.multiple_of(base[g // 4] + TILE * (g % 4), 8)
            compact[pl.ds(at, TILE), :] = part
        x = compact[...].astype(jnp.bfloat16)
        k = dot(x, wk_ref[...]).astype(jnp.bfloat16)
        keys[...] = k
        next_values[...] = dot(wv_ref[...], x, NT).astype(jnp.bfloat16)
        head_of = [lax.broadcasted_iota(jnp.int32, (128, 128), a) // 32 for a in range(2)]
        same_head = (head_of[0] == head_of[1]).astype(jnp.bfloat16)
        k_norm = jnp.max(dot(k * k, same_head))
        q_norm = jnp.float32(0.0)

        scale = jnp.float32(LOG2E / math.sqrt(32.0))
        for t in range(9):
            if t < 8:
                xt = natural[BLOCK * t : BLOCK * t + 128, :]
            else:
                xt = jnp.concatenate(
                    [natural[BLOCK * c + 128 : BLOCK * c + BLOCK, :] for c in range(8)], axis=0
                )
            qg = dot(wqg_ref[...], xt.astype(jnp.bfloat16), NT).astype(jnp.bfloat16)
            qg = qg.astype(jnp.float32)
            next_gate[:, 128 * t : 128 * t + 128] = 1.0 / (1.0 + jnp.exp(-qg[64:]))
            q = qg[:64] * scale
            high = q.astype(jnp.bfloat16)
            low = (q - high.astype(jnp.float32)).astype(jnp.bfloat16)
            for h in range(2):
                of_head = q[32 * h : 32 * h + 32]
                q_norm = jnp.maximum(
                    q_norm, jnp.max(jnp.sum(of_head * of_head, axis=0, keepdims=True))
                )
                job, half = place_of(h, t)
                lanes = slice(128 * half, 128 * half + 128)
                d = slice(32 * h, 32 * h + 32)
                q_blocks[job, 32 * h : 32 * h + 32, lanes] = high[d]
                q_blocks[job, 64 + 32 * h : 96 + 32 * h, lanes] = low[d]
        small_ref[0] = (q_norm * k_norm < 3000.0).astype(jnp.int32)

    @pl.when(step == QUARTERS - 1)
    def _():
        prepare()

    @pl.when(step >= QUARTERS)
    def _():
        small = small_ref[0] > 0
        values_t[...] = next_values[...]
        gate[...] = next_gate[...]

        def score_pass(n, safe, jobs, bufs):
            blocks = [q_blocks[job] for job in jobs]
            pieces = [slice(p, min(p + 512, 128 * n)) for p in range(0, 128 * n, 512)]

            def scores(at, job, rows):
                return dot(keys[rows, :], blocks[at]) + bias[job, rows, :]

            peaks = [jnp.full((1, 256), -jnp.inf, jnp.float32) for _ in jobs]
            if safe:
                for rows in pieces:
                    for at, job in enumerate(jobs):
                        peak = jnp.max(scores(at, job, rows), axis=0, keepdims=True)
                        peaks[at] = jnp.maximum(peaks[at], peak)
            totals = [jnp.zeros((8, 256), jnp.float32) for _ in jobs]
            for rows in pieces:
                for at, job in enumerate(jobs):
                    e = scores(at, job, rows)
                    if safe:
                        e = e - peaks[at]
                    e = jnp.exp2(e)
                    exps[bufs[at], rows, :] = e
                    totals[at] = totals[at] + jnp.sum(e.reshape(-1, 8, 256), axis=0)
            for at, buf in enumerate(bufs):
                total = jnp.sum(totals[at], axis=0, keepdims=True)
                inverse[buf] = jnp.broadcast_to(1.0 / total, (8, 256))

        def value_pass(n, bufs):
            totals = [jnp.zeros((64, 256), jnp.float32) for _ in bufs]
            for p in range(0, 128 * n, 512):
                rows = slice(p, min(p + 512, 128 * n))
                for at, buf in enumerate(bufs):
                    w = (exps[buf, rows, :] * inverse[buf][0:1]).astype(jnp.bfloat16)
                    totals[at] = totals[at] + dot(values_t[:, rows], w)
            return totals

        def mixed(total):
            return jnp.concatenate([total[:32, :128], total[32:, 128:]], axis=1)

        def heads_out(n, jobs, bufs):
            for job, total in zip(jobs, value_pass(n, bufs)):
                if job == JOBS - 1:
                    attended[job] = mixed(total)
                else:
                    attended[job] = total[32:] if job >= 4 else total[:32]

        def finish():
            for t in range(9):
                tile = slice(128 * t, 128 * t + 128)
                parts = []
                for h in range(2):
                    job, half = place_of(h, t)
                    parts.append(attended[job, :, 128 * half : 128 * half + 128])
                gated = (gate[:, tile] * jnp.concatenate(parts, axis=0)).astype(jnp.bfloat16)
                if not last:
                    out_ref[0, :, tile] = gated
                    continue
                gated = jnp.concatenate([earlier_ref[0, :, tile], gated], axis=0)
                update = dot(gated, wo_ref[...], TN)
                if t < 8:
                    result[BLOCK * t : BLOCK * t + 128, :] = update
                else:
                    for c in range(8):
                        result[BLOCK * c + 128 : BLOCK * c + BLOCK, :] = update[16 * c : 16 * c + 16]
            if last:
                for g in range(GROUPS):
                    out_ref[g, 0] = result[TILE * g : TILE * g + TILE, :].astype(jnp.bfloat16)

        def run(n):
            score_pass(n, False, (0, 1, 2), (0, 1, 2))
            score_pass(n, False, (3, 4, 5), (3, 4, 5))
            heads_out(n, (0, 1, 2), (0, 1, 2))
            score_pass(n, False, (6, 7, 8), (0, 1, 2))
            prepare()
            heads_out(n, (3, 4, 5), (3, 4, 5))
            heads_out(n, (6, 7, 8), (0, 1, 2))
            finish()

        def run_safe():
            def one(job, carry):
                score_pass(9, True, (job,), (0,))
                total = value_pass(9, (0,))[0]
                one_head = jnp.where(job >= 4, total[32:], total[:32])
                attended[job] = jnp.where(job == JOBS - 1, mixed(total), one_head)
                return carry

            lax.fori_loop(0, JOBS, one, 0)
            prepare()
            finish()

        for n in range(5, 10):
            pl.when(jnp.logical_and(chunks == n, small))(functools.partial(run, n))
        pl.when(jnp.logical_not(small))(run_safe)


def attend(first_head, columns, counts, bias, rest, x, weights, earlier=None):
    first, count = columns
    last = earlier is not None
    whole = lambda w: pl.BlockSpec(w.shape, lambda s, counts: (0,) * w.ndim)
    at = lambda s: jnp.maximum(s - QUARTERS, 0)
    ahead = lambda s: jnp.clip(s - QUARTERS + 1, 0, count - 1)
    quarter = lambda s: jnp.minimum(s, QUARTERS - 1)
    in_specs = [
        pl.BlockSpec(
            (4, 2, 1, 2, 2, 2, TILE, 128),
            lambda s, counts: (0, 0, quarter(s) // 2, quarter(s) % 2, 0, 0, 0, 0),
        ),
        pl.BlockSpec(
            (4, 2, 1, 2, 2, 1, TILE, 128),
            lambda s, counts: (0, 0, quarter(s) // 2, quarter(s) % 2, 0, 2, 0, 0),
        ),
        pl.BlockSpec((GROUPS, 1, TILE, 128), lambda s, counts: (0, first + ahead(s), 0, 0)),
    ] + [whole(w) for w in weights]
    operands = [counts, bias, rest, x, *weights]
    if last:
        in_specs.append(pl.BlockSpec((1, 64, TOKENS), lambda s, counts: (first + at(s), 0, 0)))
        operands.append(earlier)
        out_specs = pl.BlockSpec((GROUPS, 1, TILE, 128), lambda s, counts: (0, at(s), 0, 0))
        out_shape = jax.ShapeDtypeStruct((GROUPS, count, TILE, 128), jnp.bfloat16)
    else:
        out_specs = pl.BlockSpec((1, 64, TOKENS), lambda s, counts: (at(s), 0, 0))
        out_shape = jax.ShapeDtypeStruct((count, 64, TOKENS), jnp.bfloat16)
    return pl.pallas_call(
        functools.partial(attend_kernel, first_head, last),
        grid_spec=pltpu.PrefetchScalarGridSpec(
            num_scalar_prefetch=1,
            grid=(QUARTERS + count,),
            in_specs=in_specs,
            out_specs=out_specs,
            scratch_shapes=[
                pltpu.VMEM((JOBS, TOKENS, 256), jnp.float32),
                pltpu.VMEM((JOBS, 8, 256), jnp.float32),
                pltpu.VMEM((TOKENS, 128), jnp.float32),
                pltpu.VMEM((TOKENS, 128), jnp.float32),
                pltpu.VMEM((TOKENS, 128), jnp.bfloat16),
                pltpu.VMEM((64, TOKENS), jnp.bfloat16),
                pltpu.VMEM((JOBS, 128, 256), jnp.bfloat16),
                pltpu.VMEM((64, TOKENS), jnp.float32),
                pltpu.VMEM((JOBS, 32, 256), jnp.float32),
                pltpu.VMEM((6, TOKENS, 256), jnp.float32),
                pltpu.VMEM((6, 8, 256), jnp.float32),
                pltpu.VMEM((64, TOKENS), jnp.bfloat16),
                pltpu.VMEM((64, TOKENS), jnp.float32),
                pltpu.VMEM((TOKENS, 128), jnp.float32),
                pltpu.SMEM((1,), jnp.int32),
            ],
        ),
        out_shape=out_shape,
        compiler_params=pltpu.CompilerParams(vmem_limit_bytes=56 * MIB),
        cost_estimate=pl.CostEstimate(
            flops=count * 800_000_000, bytes_accessed=12_000_000, transcendentals=count * 2_400_000
        ),
        name="attend",
    )(*operands)


def head_weights(proj_weight, first_head):
    width = proj_weight.shape[0]
    part = lambda block: proj_weight[
        :, block * width + 32 * first_head : block * width + 32 * first_head + 64
    ]
    wqg = jnp.concatenate([part(0), part(3)], axis=1).T
    wk = jnp.concatenate([part(1), part(1)], axis=1)
    return [wqg, wk, part(2).T]


def key_counts(token_mask, bias_weight):
    real = jnp.sum((token_mask > 0).astype(jnp.int32).reshape(4, QUARTER), axis=1)
    bound = 25.0 * jnp.max(jnp.sum(jnp.abs(bias_weight.astype(jnp.float32)), axis=0))
    kept = jnp.where(bound < 1e8, (real + 7) // 8 * 8, QUARTER)
    return jnp.concatenate([real, kept])


ROW, COL = ("x_hi", "y", "core"), ("z", "x_lo")


def local(pair_rep, norm_gain, norm_shift, proj_weight, bias_weight, out_weight, token_mask):
    rows, cols, width = pair_rep.shape
    per_group = cols // GROUPS
    params = jnp.concatenate(
        [bias_weight.T.astype(jnp.float32), jnp.zeros((4, width), jnp.float32),
         norm_gain[None], norm_shift[None], jnp.zeros((6, width), jnp.float32)], axis=0
    )
    x, bias = norm_and_bias(pair_rep, params, 1)
    x = x.reshape(GROUPS, per_group, rows, width)
    x = lax.all_to_all(x, ROW, split_axis=0, concat_axis=0, tiled=True)
    other = lax.ppermute(bias, "x_lo", [(0, 1), (1, 0)])
    is_low = lax.axis_index("x_lo") == 0
    both = jnp.concatenate([jnp.where(is_low, bias, other), jnp.where(is_low, other, bias)], axis=0)
    bias = jnp.broadcast_to(both[None], (8,) + both.shape)
    bias = lax.all_to_all(bias, ("x_hi", "y"), split_axis=0, concat_axis=0, tiled=True)
    bias = bias.reshape(16, HEADS + 1, rows, 128)

    def gather(part):
        part = lax.all_gather(part, ("z", "core"), axis=0)
        return part.reshape(4, 2, 2, 4, 2, -1, rows, 128)

    early, late = gather(bias[:, :3]), gather(bias[:, 3:])
    counts = key_counts(token_mask, bias_weight)
    first, second = head_weights(proj_weight, 0), head_weights(proj_weight, 2)
    gated = attend(0, (0, per_group), counts, early, early, x, first)
    update = attend(2, (0, per_group), counts, late, early, x, second + [out_weight], gated)
    update = lax.all_to_all(update, ROW, split_axis=0, concat_axis=0, tiled=True)
    return place([update], rows, cols, width)


def solution(mesh):
    split = jax.sharding.Mesh(mesh.devices.reshape(2, 4, 2, 4, 2), ROW + COL)
    whole = P(ROW, COL, None)
    in_specs = (whole, P(), P(), P(), P(), P(), P())
    return jax.shard_map(local, mesh=split, in_specs=in_specs, out_specs=whole, check_vma=False)
```

```python
import functools
import math

import jax
import jax.numpy as jnp
from jax import lax
from jax.experimental import pallas as pl
from jax.experimental.pallas import tpu as pltpu
from jax.sharding import PartitionSpec as P

EPSILON = 1e-05
LOG2E = math.log2(math.e)
MASKED = -1e9 * LOG2E
HEADS = 4
MIB = 1024 * 1024

NT = (((1,), (1,)), ((), ()))
TN = (((0,), (0,)), ((), ()))


def dot(a, b, dims=(((1,), (0,)), ((), ()))):
    return lax.dot_general(a, b, dims, preferred_element_type=jnp.float32)


def layer_norm(x, gain, shift):
    x = x.astype(jnp.float32)
    x = x - jnp.mean(x, axis=-1, keepdims=True)
    spread = jnp.mean(x * x, axis=-1, keepdims=True)
    return (x * lax.rsqrt(spread + EPSILON) * gain + shift).astype(jnp.bfloat16)


def norm_kernel(x_ref, params_ref, normed_ref, bias_ref, wide, main, rest):
    step = pl.program_id(0)
    rows, cols, width = x_ref.shape
    total = normed_ref.shape[1]
    gain, shift = params_ref[8:9], params_ref[9:10]
    bw = params_ref[0:8].astype(jnp.bfloat16)

    @pl.when(step == 0)
    def _():
        rest[...] = jnp.zeros_like(rest)

    for r in range(rows):
        normed = layer_norm(x_ref[r], gain, shift)
        at = pl.multiple_of((rows * step + r) * cols, 8)
        wide[pl.ds(at, cols), :] = normed.astype(jnp.float32)
        bias = dot(bw, normed, NT)
        at = pl.ds(rows * step + r, 1)
        for h in range(HEADS):
            main[h, at, :] = bias[h : h + 1, :128]
            rest[h, at, 0:16] = bias[h : h + 1, 128:144]

    @pl.when(step == pl.num_programs(0) - 1)
    def _():
        tail = rest[0]
        for h in range(1, HEADS):
            tail = tail + pltpu.roll(rest[h], 16 * h, 1)
        slabs = [main[h].astype(jnp.bfloat16) for h in range(HEADS)]
        slabs.insert(2, tail.astype(jnp.bfloat16))
        for at, slab in enumerate(slabs):
            for copy in range(bias_ref.shape[0]):
                bias_ref[copy, at] = slab

        def col(c, carry):
            normed_ref[c] = wide[pl.ds(c, total, stride=cols), :].astype(jnp.bfloat16)
            return carry

        lax.fori_loop(0, cols, col, 0, unroll=4)


def norm_and_bias(x, params, copies):
    rows, cols, width = x.shape
    return pl.pallas_call(
        norm_kernel,
        grid=(rows // 8,),
        in_specs=[
            pl.BlockSpec((8, cols, width), lambda s: (s, 0, 0)),
            pl.BlockSpec((16, width), lambda s: (0, 0)),
        ],
        out_specs=[
            pl.BlockSpec((cols, rows, width), lambda s: (0, 0, 0)),
            pl.BlockSpec((copies, HEADS + 1, rows, 128), lambda s: (0, 0, 0, 0)),
        ],
        out_shape=[
            jax.ShapeDtypeStruct((cols, rows, width), jnp.bfloat16),
            jax.ShapeDtypeStruct((copies, HEADS + 1, rows, 128), jnp.bfloat16),
        ],
        scratch_shapes=[
            pltpu.VMEM((rows * cols, width), jnp.float32),
            pltpu.VMEM((HEADS, rows, 128), jnp.float32),
            pltpu.VMEM((HEADS, rows, 128), jnp.float32),
        ],
        compiler_params=pltpu.CompilerParams(vmem_limit_bytes=40 * MIB),
        name="norm_and_bias",
    )(x, params)


def place_kernel(*refs):
    parts, o_ref, wide = refs[:-2], refs[-2], refs[-1]
    rows, cols, width = o_ref.shape
    per_group = sum(part.shape[1] for part in parts)

    def group(g, carry):
        at = 0
        for part in parts:
            for c in range(part.shape[1]):
                start = pl.multiple_of((g * per_group + at) * rows, 8)
                wide[pl.ds(start, rows), :] = part[g, c].astype(jnp.float32)
                at += 1
        return carry

    lax.fori_loop(0, cols // per_group, group, 0)

    def row(r, carry):
        o_ref[r] = wide[pl.ds(r, cols, stride=rows), :].astype(jnp.bfloat16)
        return carry

    lax.fori_loop(0, rows, row, 0, unroll=4)


def place(parts, rows, cols, width):
    return pl.pallas_call(
        place_kernel,
        out_shape=jax.ShapeDtypeStruct((rows, cols, width), jnp.bfloat16),
        scratch_shapes=[pltpu.VMEM((rows * cols, width), jnp.float32)],
        compiler_params=pltpu.CompilerParams(vmem_limit_bytes=40 * MIB),
        name="place",
    )(*parts)


GROUPS, TILE, BLOCK = 16, 72, 144
TOKENS = GROUPS * TILE
QUARTERS = 4
QUARTER = TOKENS // QUARTERS
JOBS = 9


def place_of(h, t):
    return (4 * h + t // 2, t % 2) if t < 8 else (JOBS - 1, h)


def attend_kernel(first_head, last, counts_ref, bias_ref, rest_ref, x_ref, *refs):
    if last:
        wqg_ref, wk_ref, wv_ref, wo_ref, earlier_ref, out_ref = refs[:6]
        scratch = refs[6:]
    else:
        wqg_ref, wk_ref, wv_ref, out_ref = refs[:4]
        scratch = refs[4:]
    (bias, top, natural, compact, keys, values_t, q_blocks, gate, attended, exps,
     inverse, next_values, next_gate, result, small_ref) = scratch
    step = pl.program_id(0)
    real = [counts_ref[q] for q in range(4)]
    base = [0]
    for q in range(4):
        base.append(base[-1] + counts_ref[4 + q])
    chunks = (base[4] + 127) // 128

    @pl.when(step == 0)
    def _():
        q_blocks[...] = jnp.zeros_like(q_blocks)
        compact[...] = jnp.zeros_like(compact)
        top[...] = jnp.full_like(top, -3e38)

        def fill(job, carry):
            bias[job, QUARTER * 2 :, :] = jnp.full((QUARTER * 2, 256), MASKED, jnp.float32)
            return carry

        lax.fori_loop(0, JOBS, fill, 0)

    @pl.when(step < QUARTERS)
    def _():
        count = real[0]
        start = base[0]
        for q in range(1, QUARTERS):
            count = jnp.where(step == q, real[q], count)
            start = jnp.where(step == q, base[q], start)
        lane = lax.broadcasted_iota(jnp.int32, (TILE, 128), 1)

        for g in range(GROUPS // QUARTERS):
            at = pl.multiple_of(start + TILE * g, 8)
            position = lax.broadcasted_iota(jnp.int32, (TILE, 128), 0) + TILE * g
            keep = position < count

            def put(h, t, value):
                job, half = place_of(h, t)
                value = jnp.where(keep, value * LOG2E, MASKED)
                lanes = slice(128 * half, 128 * half + 128)
                bias[job, pl.ds(at, TILE), lanes] = value
                peak = top[job, :, lanes]
                for s in range(TILE // 8):
                    peak = jnp.maximum(peak, value[8 * s : 8 * s + 8])
                top[job, :, lanes] = peak

            for h in range(2):
                for c in range(8):
                    put(h, c, bias_ref[c // 2, g % 2, 0, g // 2, c % 2, h].astype(jnp.float32))
                tail = jnp.zeros((TILE, 128), jnp.float32)
                for c in range(8):
                    part = rest_ref[c // 2, g % 2, 0, g // 2, c % 2, 0].astype(jnp.float32)
                    shift = (16 * (c - h - first_head)) % 128
                    if shift:
                        part = pltpu.roll(part, shift, 1)
                    tail = jnp.where(lane // 16 == c, part, tail)
                put(h, 8, tail)

    @pl.when(step == QUARTERS - 1)
    def _():
        peaks = jnp.max(top[...], axis=1)

        @pl.when(jnp.max(jnp.abs(peaks)) >= 30.0)
        def _():
            def lower(job, carry):
                peak = jnp.max(top[job], axis=0, keepdims=True)
                for s in range(9):
                    rows = slice(128 * s, 128 * s + 128)
                    bias[job, rows, :] = bias[job, rows, :] - peak
                return carry

            lax.fori_loop(0, JOBS, lower, 0)

    def prepare():
        for g in range(GROUPS):
            part = x_ref[g, 0].astype(jnp.float32)
            natural[TILE * g : TILE * g + TILE, :] = part
            at = pl.multiple_of(base[g // 4] + TILE * (g % 4), 8)
            compact[pl.ds(at, TILE), :] = part
        x = compact[...].astype(jnp.bfloat16)
        k = dot(x, wk_ref[...]).astype(jnp.bfloat16)
        keys[...] = k
        next_values[...] = dot(wv_ref[...], x, NT).astype(jnp.bfloat16)
        head_of = [lax.broadcasted_iota(jnp.int32, (128, 128), a) // 32 for a in range(2)]
        same_head = (head_of[0] == head_of[1]).astype(jnp.bfloat16)
        k_norm = jnp.max(dot(k * k, same_head))
        q_norm = jnp.float32(0.0)

        scale = jnp.float32(LOG2E / math.sqrt(32.0))
        for t in range(9):
            if t < 8:
                xt = natural[BLOCK * t : BLOCK * t + 128, :]
            else:
                xt = jnp.concatenate(
                    [natural[BLOCK * c + 128 : BLOCK * c + BLOCK, :] for c in range(8)], axis=0
                )
            qg = dot(wqg_ref[...], xt.astype(jnp.bfloat16), NT).astype(jnp.bfloat16)
            qg = qg.astype(jnp.float32)
            next_gate[:, 128 * t : 128 * t + 128] = 1.0 / (1.0 + jnp.exp(-qg[64:]))
            q = qg[:64] * scale
            high = q.astype(jnp.bfloat16)
            low = (q - high.astype(jnp.float32)).astype(jnp.bfloat16)
            for h in range(2):
                of_head = q[32 * h : 32 * h + 32]
                q_norm = jnp.maximum(
                    q_norm, jnp.max(jnp.sum(of_head * of_head, axis=0, keepdims=True))
                )
                job, half = place_of(h, t)
                lanes = slice(128 * half, 128 * half + 128)
                d = slice(32 * h, 32 * h + 32)
                q_blocks[job, 32 * h : 32 * h + 32, lanes] = high[d]
                q_blocks[job, 64 + 32 * h : 96 + 32 * h, lanes] = low[d]
        small_ref[0] = (q_norm * k_norm < 3000.0).astype(jnp.int32)

    @pl.when(step == QUARTERS - 1)
    def _():
        prepare()

    @pl.when(step >= QUARTERS)
    def _():
        small = small_ref[0] > 0
        values_t[...] = next_values[...]
        gate[...] = next_gate[...]

        def score_pass(n, safe, jobs, bufs):
            blocks = [q_blocks[job] for job in jobs]
            pieces = [slice(p, min(p + 512, 128 * n)) for p in range(0, 128 * n, 512)]

            def scores(at, job, rows):
                return dot(keys[rows, :], blocks[at]) + bias[job, rows, :]

            peaks = [jnp.full((1, 256), -jnp.inf, jnp.float32) for _ in jobs]
            if safe:
                for rows in pieces:
                    for at, job in enumerate(jobs):
                        peak = jnp.max(scores(at, job, rows), axis=0, keepdims=True)
                        peaks[at] = jnp.maximum(peaks[at], peak)
            totals = [jnp.zeros((8, 256), jnp.float32) for _ in jobs]
            for rows in pieces:
                for at, job in enumerate(jobs):
                    e = scores(at, job, rows)
                    if safe:
                        e = e - peaks[at]
                    e = jnp.exp2(e)
                    exps[bufs[at], rows, :] = e
                    totals[at] = totals[at] + jnp.sum(e.reshape(-1, 8, 256), axis=0)
            for at, buf in enumerate(bufs):
                total = jnp.sum(totals[at], axis=0, keepdims=True)
                inverse[buf] = jnp.broadcast_to(1.0 / total, (8, 256))

        def value_pass(n, bufs):
            totals = [jnp.zeros((64, 256), jnp.float32) for _ in bufs]
            for p in range(0, 128 * n, 512):
                rows = slice(p, min(p + 512, 128 * n))
                for at, buf in enumerate(bufs):
                    w = (exps[buf, rows, :] * inverse[buf][0:1]).astype(jnp.bfloat16)
                    totals[at] = totals[at] + dot(values_t[:, rows], w)
            return totals

        def mixed(total):
            return jnp.concatenate([total[:32, :128], total[32:, 128:]], axis=1)

        def heads_out(n, jobs, bufs):
            for job, total in zip(jobs, value_pass(n, bufs)):
                if job == JOBS - 1:
                    attended[job] = mixed(total)
                else:
                    attended[job] = total[32:] if job >= 4 else total[:32]

        def finish():
            for t in range(9):
                tile = slice(128 * t, 128 * t + 128)
                parts = []
                for h in range(2):
                    job, half = place_of(h, t)
                    parts.append(attended[job, :, 128 * half : 128 * half + 128])
                gated = (gate[:, tile] * jnp.concatenate(parts, axis=0)).astype(jnp.bfloat16)
                if not last:
                    out_ref[0, :, tile] = gated
                    continue
                gated = jnp.concatenate([earlier_ref[0, :, tile], gated], axis=0)
                update = dot(gated, wo_ref[...], TN)
                if t < 8:
                    result[BLOCK * t : BLOCK * t + 128, :] = update
                else:
                    for c in range(8):
                        result[BLOCK * c + 128 : BLOCK * c + BLOCK, :] = update[16 * c : 16 * c + 16]
            if last:
                for g in range(GROUPS):
                    out_ref[g, 0] = result[TILE * g : TILE * g + TILE, :].astype(jnp.bfloat16)

        def run(n):
            score_pass(n, False, (0, 1, 2), (0, 1, 2))
            score_pass(n, False, (3, 4, 5), (3, 4, 5))
            heads_out(n, (0, 1, 2), (0, 1, 2))
            score_pass(n, False, (6, 7, 8), (0, 1, 2))
            prepare()
            heads_out(n, (3, 4, 5), (3, 4, 5))
            heads_out(n, (6, 7, 8), (0, 1, 2))
            finish()

        def run_safe():
            def one(job, carry):
                score_pass(9, True, (job,), (0,))
                total = value_pass(9, (0,))[0]
                one_head = jnp.where(job >= 4, total[32:], total[:32])
                attended[job] = jnp.where(job == JOBS - 1, mixed(total), one_head)
                return carry

            lax.fori_loop(0, JOBS, one, 0)
            prepare()
            finish()

        for n in range(5, 10):
            pl.when(jnp.logical_and(chunks == n, small))(functools.partial(run, n))
        pl.when(jnp.logical_not(small))(run_safe)


def attend(first_head, columns, counts, bias, rest, x, weights, earlier=None):
    first, count = columns
    last = earlier is not None
    whole = lambda w: pl.BlockSpec(w.shape, lambda s, counts: (0,) * w.ndim)
    at = lambda s: jnp.maximum(s - QUARTERS, 0)
    ahead = lambda s: jnp.clip(s - QUARTERS + 1, 0, count - 1)
    quarter = lambda s: jnp.minimum(s, QUARTERS - 1)
    in_specs = [
        pl.BlockSpec(
            (4, 2, 1, 2, 2, 2, TILE, 128),
            lambda s, counts: (0, 0, quarter(s) // 2, quarter(s) % 2, 0, 0, 0, 0),
        ),
        pl.BlockSpec(
            (4, 2, 1, 2, 2, 1, TILE, 128),
            lambda s, counts: (0, 0, quarter(s) // 2, quarter(s) % 2, 0, 2, 0, 0),
        ),
        pl.BlockSpec((GROUPS, 1, TILE, 128), lambda s, counts: (0, first + ahead(s), 0, 0)),
    ] + [whole(w) for w in weights]
    operands = [counts, bias, rest, x, *weights]
    if last:
        in_specs.append(pl.BlockSpec((1, 64, TOKENS), lambda s, counts: (first + at(s), 0, 0)))
        operands.append(earlier)
        out_specs = pl.BlockSpec((GROUPS, 1, TILE, 128), lambda s, counts: (0, at(s), 0, 0))
        out_shape = jax.ShapeDtypeStruct((GROUPS, count, TILE, 128), jnp.bfloat16)
    else:
        out_specs = pl.BlockSpec((1, 64, TOKENS), lambda s, counts: (at(s), 0, 0))
        out_shape = jax.ShapeDtypeStruct((count, 64, TOKENS), jnp.bfloat16)
    return pl.pallas_call(
        functools.partial(attend_kernel, first_head, last),
        grid_spec=pltpu.PrefetchScalarGridSpec(
            num_scalar_prefetch=1,
            grid=(QUARTERS + count,),
            in_specs=in_specs,
            out_specs=out_specs,
            scratch_shapes=[
                pltpu.VMEM((JOBS, TOKENS, 256), jnp.float32),
                pltpu.VMEM((JOBS, 8, 256), jnp.float32),
                pltpu.VMEM((TOKENS, 128), jnp.float32),
                pltpu.VMEM((TOKENS, 128), jnp.float32),
                pltpu.VMEM((TOKENS, 128), jnp.bfloat16),
                pltpu.VMEM((64, TOKENS), jnp.bfloat16),
                pltpu.VMEM((JOBS, 128, 256), jnp.bfloat16),
                pltpu.VMEM((64, TOKENS), jnp.float32),
                pltpu.VMEM((JOBS, 32, 256), jnp.float32),
                pltpu.VMEM((6, TOKENS, 256), jnp.float32),
                pltpu.VMEM((6, 8, 256), jnp.float32),
                pltpu.VMEM((64, TOKENS), jnp.bfloat16),
                pltpu.VMEM((64, TOKENS), jnp.float32),
                pltpu.VMEM((TOKENS, 128), jnp.float32),
                pltpu.SMEM((1,), jnp.int32),
            ],
        ),
        out_shape=out_shape,
        compiler_params=pltpu.CompilerParams(vmem_limit_bytes=56 * MIB),
        cost_estimate=pl.CostEstimate(
            flops=count * 800_000_000, bytes_accessed=12_000_000, transcendentals=count * 2_400_000
        ),
        name="attend",
    )(*operands)


def head_weights(proj_weight, first_head):
    width = proj_weight.shape[0]
    part = lambda block: proj_weight[
        :, block * width + 32 * first_head : block * width + 32 * first_head + 64
    ]
    wqg = jnp.concatenate([part(0), part(3)], axis=1).T
    wk = jnp.concatenate([part(1), part(1)], axis=1)
    return [wqg, wk, part(2).T]


def key_counts(token_mask, bias_weight):
    real = jnp.sum((token_mask > 0).astype(jnp.int32).reshape(4, QUARTER), axis=1)
    bound = 25.0 * jnp.max(jnp.sum(jnp.abs(bias_weight.astype(jnp.float32)), axis=0))
    kept = jnp.where(bound < 1e8, (real + 7) // 8 * 8, QUARTER)
    return jnp.concatenate([real, kept])


ROW, COL = ("x_hi", "y", "core"), ("z", "x_lo")


def local(pair_rep, norm_gain, norm_shift, proj_weight, bias_weight, out_weight, token_mask):
    rows, cols, width = pair_rep.shape
    per_group = cols // GROUPS
    params = jnp.concatenate(
        [bias_weight.T.astype(jnp.float32), jnp.zeros((4, width), jnp.float32),
         norm_gain[None], norm_shift[None], jnp.zeros((6, width), jnp.float32)], axis=0
    )
    x, bias = norm_and_bias(pair_rep, params, 16)
    x = x.reshape(GROUPS, per_group, rows, width)
    x = lax.all_to_all(x, ROW, split_axis=0, concat_axis=0, tiled=True)
    bias = lax.all_to_all(bias, ("x_hi", "y", "x_lo"), split_axis=0, concat_axis=0, tiled=True)

    def gather(part):
        part = lax.all_gather(part, ("z", "core"), axis=0)
        return part.reshape(4, 2, 2, 4, 2, -1, rows, 128)

    early, late = gather(bias[:, :3]), gather(bias[:, 3:])
    counts = key_counts(token_mask, bias_weight)
    first, second = head_weights(proj_weight, 0), head_weights(proj_weight, 2)
    gated = attend(0, (0, per_group), counts, early, early, x, first)
    update = attend(2, (0, per_group), counts, late, early, x, second + [out_weight], gated)
    update = lax.all_to_all(update, ROW, split_axis=0, concat_axis=0, tiled=True)
    return place([update], rows, cols, width)


def solution(mesh):
    split = jax.sharding.Mesh(mesh.devices.reshape(2, 4, 2, 4, 2), ROW + COL)
    whole = P(ROW, COL, None)
    in_specs = (whole, P(), P(), P(), P(), P(), P())
    return jax.shard_map(local, mesh=split, in_specs=in_specs, out_specs=whole, check_vma=False)
```
